512 devices in a mesh: dp: 8 (over y, core), vocab: 64 (over z, x).
Axes of the slice: x: 4, y: 4, z: 16, core: 2. Of those that a mesh axis runs over, the one named last changes fastest.
Arguments:
- hidden: bfloat16 [384, 4096], P('dp'), may hold values from -30 to 30
- head_weight: bfloat16 [131072, 4096], P('vocab', 'dp'), may hold values from -0.375 to 0.375
- teacher_ids: int32 [384, 256], P('dp'), may hold values from 0 to 131071
- teacher_logits: float32 [384, 256], P('dp'), may hold values from -16 to 16
Outputs:
- hidden_grad: bfloat16 [384, 4096], P('dp', 'vocab')
- head_grad: bfloat16 [131072, 4096], P('vocab', 'dp')
- loss: float32 [], replicated
The draws below stay inside these ranges and needn't reach their ends.
All inputs are finite; a program needn't handle non-finite values.
Results may differ from the reference program's by a relative error of at most 0.0049.
Values may be sent and summed in bfloat16 or wider, within the bound.
A program may use at most 64 MiB of HBM per device.

```python
import math
import jax
import jax.numpy as jnp

D = 4096
K = 256
TOKENS = 384
V = 131072


def draw_hidden(key, part):
    key = jax.random.fold_in(key, 11)
    first, second = jax.random.split(key, 2)
    scales = jnp.exp(jax.random.uniform(second, (TOKENS, 1), jnp.float32, math.log(0.5), math.log(5.0)))
    values = jnp.clip(jax.random.normal(first, (TOKENS, D), jnp.float32), -6.0, 6.0) * scales
    return values.astype(jnp.bfloat16)


def set_ends(drawn, key, least, high):
    place = [jax.random.randint(jax.random.fold_in(key, axis), (), 0, length) for axis, length in enumerate(drawn.shape)]
    longest = drawn.shape.index(max(drawn.shape))
    next_to = place[:longest] + [(place[longest] + 1) % drawn.shape[longest]] + place[longest + 1:]
    return drawn.at[tuple(place)].set(least).at[tuple(next_to)].set(high)


def strengthened(array, own_key, source, target, blocks, factor):
    owner, partner = [(jnp.arange(array.shape[position]) // (array.shape[position] // blocks)).reshape([-1 if axis == position else 1 for axis in range(array.ndim)]) for position in (source, target)]
    chosen = jax.random.permutation(own_key, blocks)[partner]
    strong = (owner == chosen) | (owner == (partner + blocks // 2) % blocks)
    return jnp.where(strong, factor * array, array)


def block_levels(stream_key, dims, cuts, smallest, top_value):
    def one(axis_at, blocks):
        steps = jax.random.uniform(jax.random.fold_in(jax.random.fold_in(stream_key, 6), axis_at), (blocks,), jnp.float32, smallest / len(cuts), top_value / len(cuts))
        return jnp.repeat(jnp.exp(steps), dims[axis_at] // blocks).reshape((-1,) + (1,) * (len(dims) - axis_at - 1))

    factor_of = one(*cuts[0])
    for cut in cuts[1:]:
        factor_of = factor_of * one(*cut)
    return factor_of


def gaussian(own_key, dims, scale, reach, cuts=(), kind=jnp.bfloat16):
    array = scale * jax.random.normal(own_key, dims, jnp.float32)
    if cuts:
        array = array * block_levels(own_key, dims, cuts, -0.22, 0.18)
    return jnp.clip(array, -reach, reach).astype(kind)


def noise_with(key, dims, scale, reach, cuts, heavy, kind=jnp.bfloat16):
    entries = scale * jax.random.normal(key, dims, jnp.float32)
    if cuts:
        entries = entries * block_levels(key, dims, cuts, -0.22, 0.18)
    return jnp.clip(strengthened(entries, jax.random.fold_in(key, 3), *heavy), -reach, reach).astype(kind)


def setup_inputs(seed: int = 0) -> dict:
    splits = jax.random.split(jax.random.key(seed), 5)
    hidden = draw_hidden(jax.random.fold_in(splits[4], 71), 0)
    head_weight = noise_with(splits[1], (V, D), (1.5 / D ** 0.5), 0.375, ((0, 64), (1, 8)), (0, 1, 64, 4.0))
    teacher_ids = set_ends(jax.random.randint(splits[2], (TOKENS, K), 0, V), jax.random.fold_in(splits[2], 1), 0, V - 1).astype(jnp.int32)
    teacher_logits = gaussian(splits[3], (TOKENS, K), 4.0, 16.0, ((0, 8),), jnp.float32)
    return {"hidden": hidden, "head_weight": head_weight, "teacher_ids": teacher_ids, "teacher_logits": teacher_logits}


soft_cap = 30.0


def reference(hidden, head_weight, teacher_ids, teacher_logits):
    raw = jnp.dot(hidden, head_weight.T, preferred_element_type=jnp.float32)
    squash = jnp.tanh(raw / soft_cap)
    student = soft_cap * squash
    expo = jnp.exp(student)
    total = jnp.sum(expo, axis=1)
    teacher_logp = teacher_logits - jnp.log(jnp.sum(jnp.exp(teacher_logits), axis=1, keepdims=True))
    teacher_prob = jnp.exp(teacher_logp)
    row_index = jnp.broadcast_to(jnp.arange(teacher_ids.shape[0], dtype=jnp.int32)[:, None], teacher_ids.shape)
    target = jnp.zeros(raw.shape, raw.dtype).at[row_index, teacher_ids].add(teacher_prob)
    cross = jnp.sum(target * student, axis=1)
    loss = jnp.mean(jnp.sum(teacher_prob * teacher_logp, axis=1) - cross + jnp.log(total))
    grad_raw = ((expo / total[:, None] - target) * (1.0 - squash * squash)).astype(jnp.bfloat16)
    hidden_grad = jnp.dot(grad_raw, head_weight, preferred_element_type=jnp.float32).astype(jnp.bfloat16)
    head_grad = jnp.dot(grad_raw.T, hidden, preferred_element_type=jnp.float32).astype(jnp.bfloat16)
    return hidden_grad, head_grad, loss
```

```python
import jax
import jax.numpy as jnp
from jax import lax
from jax.experimental import pallas as pl
from jax.experimental.pallas import tpu as pltpu
from jax.sharding import PartitionSpec as P

MESH = pl.DeviceIdType.MESH
F32 = jnp.float32
BF16 = jnp.bfloat16
soft_cap = 30.0

NY, NC, NX, NZ = 4, 2, 4, 16
TOK, D, K = 48, 4096, 256
FEAT = D // 8
VOCAB = 131072 // 64
NQ = 4
QC = VOCAB // NQ
NHI = VOCAB // 128
BEND = 48.0
LEVELS = 32767.0


def encode(x):
    return jnp.round(x * (LEVELS / (jnp.abs(x) + BEND))).astype(jnp.int32).astype(jnp.int16)


def decode(q):
    u = q.astype(jnp.int32).astype(F32)
    return u * (BEND / (LEVELS - jnp.abs(u)))


def mm(a, b, ca, cb):
    return lax.dot_general(a, b, (((ca,), (cb,)), ((), ())), preferred_element_type=F32)


def kernel(
    hidden, weight, ids, logits, out_hidden, out_head, out_loss,
    wv, hv, psib, pown, srecv, enc_opp, enc_nb, in_opp, in_nb,
    prob, tgt, es, om, psx, psz, lossb, gv, gt, xs, xr, zs, zr, fin, fin_in, head,
    w_sem, own_sem, hs_sem, hr_sem, ss_sem, sr_sem, rs_s, rs_r,
    px_s, px_r, pz_s, pz_r, ls_s, ls_r, ag_s, ag_r, x_s, x_r, z_s, z_r, f_s, f_r, head_sem,
):
    me = lax.axis_index("dp")
    vo = lax.axis_index("vocab")
    y, c = me // 2, me % 2
    z, x = vo // NX, vo % NX

    def dp_dev(o, cx):
        return {"dp": ((y + o) % NY) * 2 + (c + cx) % 2, "vocab": vo}

    def x_dev(r):
        return {"dp": me, "vocab": z * NX + (x + r) % NX}

    def z_dev(zz):
        return {"dp": me, "vocab": zz * NX + x}

    def rc(src, dst, ssem, rsem, dev):
        return pltpu.make_async_remote_copy(
            src_ref=src, dst_ref=dst, send_sem=ssem, recv_sem=rsem, device_id=dev, device_id_type=MESH
        )

    waits = []

    def send(src, dst, ssem, rsem, dev):
        copy = rc(src, dst, ssem, rsem, dev)
        copy.start()
        waits.append(copy)

    def wait_recv(dst, ssem, rsem):
        rc(dst, dst, ssem, rsem, dp_dev(0, 1)).wait_recv()

    sends_final = z % 2 == c
    fin_block = z // 2
    dest_v = [8 * me + 2 * x + h for h in range(2)]
    dest_self = [jnp.logical_and(fin_block == me, v == vo) for v in dest_v]
    src_dp = vo // 8
    src_v = (2 * me + src_dp % 2) * NX + (vo % 8) // 2
    src_self = jnp.logical_and(src_dp == me, src_v == vo)

    wcopies = []
    for q in range(NQ):
        rows = pl.ds(q * QC, QC)
        wcopies.append(pltpu.make_async_copy(weight.at[rows], wv.at[rows], w_sem.at[q]))
    own_h = pltpu.make_async_copy(hidden.at[:, pl.ds(pl.multiple_of(me * FEAT, FEAT), FEAT)], hv.at[0, 0], own_sem)
    own_h.start()
    for w in wcopies:
        w.start()

    barrier = pltpu.get_barrier_semaphore()

    def greet(dev):
        pl.semaphore_signal(barrier, inc=1, device_id=dev, device_id_type=MESH)

    for o in range(NY):
        for cx in range(NC):
            if o or cx:
                greet(dp_dev(o, cx))
    for r in range(1, NX):
        greet(x_dev(r))
    for r in range(1, NZ):
        greet(z_dev((z + r) % NZ))

    @pl.when(jnp.logical_not(src_self))
    def _():
        greet({"dp": src_dp, "vocab": src_v})

    extra = jnp.where(
        sends_final, 2 - dest_self[0].astype(jnp.int32) - dest_self[1].astype(jnp.int32), 0
    )
    pl.semaphore_wait(barrier, 7 + (NX - 1) + (NZ - 1) + extra)

    for o, cx in ((2, 0), (2, 1), (1, 0), (3, 0), (1, 1), (3, 1), (0, 1)):
        dev = dp_dev(o, cx)
        back = (-o) % NY
        cols = pl.ds(pl.multiple_of(dev["dp"] * FEAT, FEAT), FEAT)
        send(hidden.at[:, cols], hv.at[back, cx], hs_sem.at[o, cx], hr_sem.at[back, cx], dev)

    lg = logits[...]
    logp = lg - jnp.log(jnp.sum(jnp.exp(lg), axis=1, keepdims=True))
    pr = jnp.exp(logp)
    prob[...] = pr
    entropy = jnp.sum(pr * logp, axis=1, keepdims=True)

    for q in range(NQ):
        wcopies[q].wait()
    for o in range(NY):
        wait_recv(hv.at[o, 1], hs_sem.at[o, 1], hr_sem.at[o, 1])

    def q_of(s):
        return (s % 2) * 2 + s // 2

    def sib_copy(q):
        return rc(psib.at[q], srecv.at[q], ss_sem.at[q], sr_sem.at[q], dp_dev(0, 1))

    @pl.loop(0, NQ)
    def _(s):
        q = q_of(s)
        hb = hv[:, 1].reshape(NY * TOK, FEAT)
        part = mm(hb, wv[pl.ds(pl.multiple_of(q * QC, QC), QC), :], 1, 1)
        psib[q] = part.reshape(NY, TOK, QC)
        sib_copy(q).start()

    own_h.wait()
    for o in range(1, NY):
        wait_recv(hv.at[o, 0], hs_sem.at[o, 0], hr_sem.at[o, 0])

    def way(q):
        return 1 + 2 * (q // 2)

    def opp_copy(q):
        return rc(enc_opp.at[q], in_opp.at[q], rs_s.at[0, q], rs_r.at[0, q], dp_dev(way(q), 0))

    def nb_copy(q, o):
        slot, back = o // 2, 1 - o // 2
        return rc(enc_nb.at[q, slot], in_nb.at[q, back], rs_s.at[1 + slot, q], rs_r.at[1 + back, q], dp_dev(o, 0))

    @pl.loop(0, NQ)
    def _(s):
        q = q_of(s)
        hb = hv[:, 0].reshape(NY * TOK, FEAT)
        part = mm(hb, wv[pl.ds(pl.multiple_of(q * QC, QC), QC), :], 1, 1)
        pown[q] = part.reshape(NY, TOK, QC)
        wait_recv(srecv.at[q], ss_sem.at[q], sr_sem.at[q])
        enc_opp[q] = encode(pown[q, 2] + srecv[q, 2])
        opp_copy(q).start()
        other = 4 - way(q)
        enc_nb[q, other // 2] = encode(pown[q, other] + srecv[q, other])
        nb_copy(q, other).start()

    @pl.loop(0, NQ)
    def _(s):
        q = q_of(s)
        wait_recv(in_opp.at[q], rs_s.at[0, q], rs_r.at[0, q])
        o = way(q)
        enc_nb[q, o // 2] = encode(pown[q, o] + srecv[q, o] + decode(in_opp[q]))
        nb_copy(q, o).start()

    first = vo * VOCAB
    rows16 = lax.broadcasted_iota(jnp.int32, (NHI, K), 0)
    rows128 = lax.broadcasted_iota(jnp.int32, (128, K), 0)

    @pl.loop(0, TOK)
    def _(t):
        place = ids[pl.ds(t, 1), :] - first
        p = prob[pl.ds(t, 1), :]
        a = jnp.where((place >> 7) == rows16, p, 0.0)
        a1 = a.astype(BF16)
        rest = a - a1.astype(F32)
        a2 = rest.astype(BF16)
        a3 = (rest - a2.astype(F32)).astype(BF16)
        b = jnp.where((place & 127) == rows128, 1.0, 0.0).astype(BF16)
        both = mm(jnp.concatenate([a1, a2, a3], axis=0), b, 1, 1)
        tgt[t] = both[0:NHI] + both[NHI:2 * NHI] + both[2 * NHI:3 * NHI]

    tot = jnp.zeros((TOK, 128), F32)
    crs = jnp.zeros((TOK, 128), F32)
    for s in range(NQ):
        q = q_of(s)
        for slot in range(2):
            wait_recv(in_nb.at[q, slot], rs_s.at[1 + slot, q], rs_r.at[1 + slot, q])
        for k in range(QC // 128):
            cols = slice(k * 128, (k + 1) * 128)
            hi = q * (QC // 128) + k
            raw = (
                pown[q, 0, :, cols] + srecv[q, 0, :, cols]
                + decode(in_nb[q, 0, :, cols]) + decode(in_nb[q, 1, :, cols])
            )
            squash = jnp.tanh(raw * (1.0 / soft_cap))
            student = soft_cap * squash
            expo = jnp.exp(student)
            es[hi] = expo
            om[hi] = 1.0 - squash * squash
            tot = tot + expo
            crs = crs + tgt[:, hi, :] * student

    lane = lax.broadcasted_iota(jnp.int32, (TOK, 128), 1)
    row = lax.broadcasted_iota(jnp.int32, (TOK, 128), 0)
    mine = jnp.where(lane == row, jnp.sum(tot, axis=1, keepdims=True), 0.0) + jnp.where(
        lane == row + 64, jnp.sum(crs, axis=1, keepdims=True), 0.0
    )
    psx[x] = jnp.sum(mine, axis=0, keepdims=True)
    for r in range(1, NX):
        send(psx.at[x], psx.at[x], px_s.at[r], px_r.at[x], x_dev(r))
    for r in range(1, NX):
        src = (x + r) % NX
        wait_recv(psx.at[src], px_s.at[r], px_r.at[src])
    psz[z] = psx[0] + psx[1] + psx[2] + psx[3]
    for r in range(1, NZ):
        send(psz.at[z], psz.at[z], pz_s.at[r], pz_r.at[z], z_dev((z + r) % NZ))
    for r in range(1, NZ):
        src = (z + r) % NZ
        wait_recv(psz.at[src], pz_s.at[r], pz_r.at[src])
    sums = psz[0]
    for k in range(1, NZ):
        sums = sums + psz[k]
    sums = jnp.broadcast_to(sums, (TOK, 128))
    total = jnp.sum(jnp.where(lane == row, sums, 0.0), axis=1, keepdims=True)
    cross = jnp.sum(jnp.where(lane == row + 64, sums, 0.0), axis=1, keepdims=True)
    inv = 1.0 / total
    for hi in range(NHI):
        g = (es[hi] * inv - tgt[:, hi, :]) * om[hi]
        gv[0, 0, :, hi * 128:(hi + 1) * 128] = g.astype(BF16)

    half = [pl.ds(0, VOCAB // 2), pl.ds(VOCAB // 2, VOCAB // 2)]

    def pass_on(n, o, h, do, dcx):
        back = (o - do) % NY
        src = gv.at[o, 0] if h is None else gv.at[o, 0, :, half[h]]
        dst = gv.at[back, dcx] if h is None else gv.at[back, dcx, :, half[h]]
        send(src, dst, ag_s.at[n], ag_r.at[n], dp_dev(do, dcx))

    def arrived(n, o, cx, h):
        dst = gv.at[o, cx] if h is None else gv.at[o, cx, :, half[h]]
        wait_recv(dst, ag_s.at[n], ag_r.at[n])

    pass_on(0, 0, 0, 1, 0)
    pass_on(1, 0, 1, 3, 0)
    pass_on(2, 0, None, 0, 1)
    pass_on(3, 0, 1, 1, 0)
    pass_on(4, 0, 0, 3, 0)

    token_loss = entropy - cross + jnp.log(total)
    lossb[me] = jnp.broadcast_to(jnp.sum(token_loss, axis=0, keepdims=True), (1, 128))
    for o in range(NY):
        for cx in range(NC):
            if o or cx:
                dev = dp_dev(o, cx)
                send(lossb.at[me], lossb.at[me], ls_s.at[o * 2 + cx], ls_r.at[me], dev)

    def terms(o):
        ga = gv[o].reshape(2 * TOK, VOCAB)
        for n in range(2):
            part = mm(ga, wv[:, n * 256:(n + 1) * 256], 1, 0)
            for m in range(2):
                piece = part[:, m * 128:(m + 1) * 128]
                gt[o, 2 * n + m] = piece
                xs[o, 2 * n + m] = piece.astype(BF16)
        for r in range(1, NX):
            there = (x + r) % NX
            send(xs.at[o, there], xr.at[o, (-r) % NX - 1], x_s.at[o, r - 1], x_r.at[o, (-r) % NX - 1], x_dev(r))

    zsends = []

    def to_z(o):
        for r in range(NX - 1):
            wait_recv(xr.at[o, r], x_s.at[o, r], x_r.at[o, r])
        val = gt[o, x]
        for r in range(NX - 1):
            val = val + xr[o, r].astype(F32)
        for cx in range(NC):
            i = ((y + o) % NY) * 2 + (c + cx) % 2
            zd = 2 * i + c
            r = (z - zd + NZ) % NZ
            zs[o, cx] = val[cx * TOK:(cx + 1) * TOK].astype(BF16)
            copy = rc(zs.at[o, cx], zr.at[r], z_s.at[o, cx], z_r.at[r], z_dev(zd))

            @pl.when(r != 0)
            def _():
                copy.start()

            zsends.append((r, copy))

            @pl.when(r == 0)
            def _():
                zr[0] = zs[o, cx]

    arrived(2, 0, 1, None)
    terms(0)
    arrived(0, 3, 0, 0)
    pass_on(5, 3, 0, 1, 0)
    pass_on(7, 3, 0, 0, 1)
    arrived(1, 1, 0, 1)
    pass_on(6, 1, 1, 3, 0)
    pass_on(8, 1, 1, 0, 1)
    arrived(3, 3, 0, 1)
    pass_on(9, 3, 1, 0, 1)
    arrived(4, 1, 0, 0)
    pass_on(10, 1, 0, 0, 1)
    arrived(8, 1, 1, 1)
    arrived(10, 1, 1, 0)
    terms(1)
    to_z(0)
    arrived(7, 3, 1, 0)
    arrived(9, 3, 1, 1)
    terms(3)
    to_z(1)
    arrived(5, 2, 0, 0)
    pass_on(11, 2, 0, 0, 1)
    arrived(6, 2, 0, 1)
    pass_on(12, 2, 1, 0, 1)
    arrived(11, 2, 1, 0)
    arrived(12, 2, 1, 1)
    terms(2)
    to_z(3)

    HB = 256

    def head_copy(n):
        rows = pl.ds(pl.multiple_of(n * HB, HB), HB)
        return pltpu.make_async_copy(head.at[rows], out_head.at[rows], head_sem.at[n])

    def head_part(low, high):
        @pl.loop(low, high)
        def _(n):
            rows = pl.ds(pl.multiple_of(n * HB, HB), HB)
            ga = gv[:, :, :, rows].reshape(8 * TOK, HB)
            hb = hv[...].reshape(8 * TOK, FEAT)
            head[rows, :] = mm(ga, hb, 0, 0).astype(BF16)
            head_copy(n).start()

    nh = VOCAB // HB
    head_part(0, nh // 2)
    to_z(2)
    head_part(nh // 2, nh)

    @pl.when(sends_final)
    def _():
        acc = zr[0].astype(F32)
        for r in range(1, NZ):
            wait_recv(zr.at[r], f_s.at[0], z_r.at[r])
            acc = acc + zr[r].astype(F32)
        fin[...] = acc.astype(BF16)
        for h in range(2):
            copy = rc(fin, fin_in, f_s.at[h], f_r, {"dp": fin_block, "vocab": dest_v[h]})

            @pl.when(jnp.logical_not(dest_self[h]))
            def _():
                copy.start()

            @pl.when(dest_self[h])
            def _():
                fin_in[...] = fin[...]

    for o in range(NY):
        for cx in range(NC):
            if o or cx:
                src = dp_dev(o, cx)["dp"]
                wait_recv(lossb.at[src], ls_s.at[o * 2 + cx], ls_r.at[src])
    loss = lossb[0]
    for k in range(1, 8):
        loss = loss + lossb[k]
    out_loss[...] = loss * (1.0 / (8 * TOK))

    @pl.when(jnp.logical_not(src_self))
    def _():
        wait_recv(fin_in, f_s.at[0], f_r)

    both = fin_in[...].astype(F32)
    out_hidden[...] = jnp.where(vo % 2 == 0, both[:, :64], both[:, 64:]).astype(BF16)

    for copy in waits:
        copy.wait_send()

    @pl.loop(0, NQ)
    def _(q):
        sib_copy(q).wait_send()
        opp_copy(q).wait_send()
        nb_copy(q, 1).wait_send()
        nb_copy(q, 3).wait_send()

    for r, copy in zsends:
        @pl.when(r != 0)
        def _():
            copy.wait_send()

    @pl.when(sends_final)
    def _():
        for h in range(2):
            @pl.when(jnp.logical_not(dest_self[h]))
            def _():
                rc(fin, fin_in, f_s.at[h], f_r, {"dp": fin_block, "vocab": dest_v[h]}).wait_send()

    @pl.loop(0, nh)
    def _(n):
        head_copy(n).wait()


def per_device(hidden, head_weight, teacher_ids, teacher_logits):
    vm = pltpu.VMEM
    dma = pltpu.SemaphoreType.DMA
    scratch = [
        vm((VOCAB, FEAT), BF16),
        vm((NY, NC, TOK, FEAT), BF16),
        vm((NQ, NY, TOK, QC), F32),
        vm((NQ, NY, TOK, QC), F32),
        vm((NQ, NY, TOK, QC), F32),
        vm((NQ, TOK, QC), jnp.int16),
        vm((NQ, 2, TOK, QC), jnp.int16),
        vm((NQ, TOK, QC), jnp.int16),
        vm((NQ, 2, TOK, QC), jnp.int16),
        vm((TOK, K), F32),
        vm((TOK, NHI, 128), F32),
        vm((NHI, TOK, 128), F32),
        vm((NHI, TOK, 128), F32),
        vm((NX, 1, 128), F32),
        vm((NZ, 1, 128), F32),
        vm((8, 1, 128), F32),
        vm((NY, NC, TOK, VOCAB), BF16),
        vm((NY, NX, 2 * TOK, 128), F32),
        vm((NY, NX, 2 * TOK, 128), BF16),
        vm((NY, NX - 1, 2 * TOK, 128), BF16),
        vm((NY, NC, TOK, 128), BF16),
        vm((NZ, TOK, 128), BF16),
        vm((TOK, 128), BF16),
        vm((TOK, 128), BF16),
        vm((VOCAB, FEAT), BF16),
        dma((NQ,)), dma, dma((NY, NC)), dma((NY, NC)), dma((NQ,)), dma((NQ,)), dma((3, NQ)), dma((3, NQ)),
        dma((NX,)), dma((NX,)), dma((NZ,)), dma((NZ,)), dma((8,)), dma((8,)), dma((13,)), dma((13,)),
        dma((NY, NX - 1)), dma((NY, NX - 1)), dma((NY, NC)), dma((NZ,)), dma((2,)), dma, dma((VOCAB // 256,)),
    ]
    anys = pl.BlockSpec(memory_space=pl.ANY)
    vmem = pl.BlockSpec(memory_space=pltpu.VMEM)
    hidden_grad, head_grad, loss = pl.pallas_call(
        kernel,
        out_shape=(
            jax.ShapeDtypeStruct((TOK, D // 64), BF16),
            jax.ShapeDtypeStruct((VOCAB, FEAT), BF16),
            jax.ShapeDtypeStruct((1, 128), F32),
        ),
        in_specs=[anys, anys, vmem, vmem],
        out_specs=(vmem, anys, vmem),
        scratch_shapes=scratch,
        compiler_params=pltpu.CompilerParams(
            collective_id=0, has_side_effects=True, vmem_limit_bytes=40 * 1024 * 1024
        ),
    )(hidden, head_weight, teacher_ids, teacher_logits)
    return hidden_grad, head_grad, loss[0, 0]


def solution(mesh):
    in_specs = (P("dp", None), P("vocab", "dp"), P("dp", None), P("dp", None))
    out_specs = (P("dp", "vocab"), P("vocab", "dp"), P())
    return jax.shard_map(
        per_device, mesh=mesh, in_specs=in_specs, out_specs=out_specs, check_vma=False
    )
```

```python
import jax
import jax.numpy as jnp
from jax import lax
from jax.experimental import pallas as pl
from jax.experimental.pallas import tpu as pltpu
from jax.sharding import PartitionSpec as P

MESH = pl.DeviceIdType.MESH
F32 = jnp.float32
BF16 = jnp.bfloat16
soft_cap = 30.0

NY, NC, NX, NZ = 4, 2, 4, 16
TOK, D, K = 48, 4096, 256
FEAT = D // 8
VOCAB = 131072 // 64
NQ = 4
QC = VOCAB // NQ
NHI = VOCAB // 128
BEND = 48.0
LEVELS = 32767.0


def encode(x):
    return jnp.round(x * (LEVELS / (jnp.abs(x) + BEND))).astype(jnp.int32).astype(jnp.int16)


def decode(q):
    u = q.astype(jnp.int32).astype(F32)
    return u * (BEND / (LEVELS - jnp.abs(u)))


def mm(a, b, ca, cb):
    return lax.dot_general(a, b, (((ca,), (cb,)), ((), ())), preferred_element_type=F32)


def kernel(
    hidden, weight, ids_in, logits_in, out_hidden, out_head, out_loss,
    ids, logits, wv, hv, psib, pown, srecv, enc_opp, enc_nb, in_opp, in_nb,
    prob, tgt, es, om, psx, psz, lossb, gv, gt, xs, xr, ys, yr, zr, fin, fin_in,
    id_sem, w_sem, own_sem, hs_sem, hr_sem, ss_sem, sr_sem, rs_s, rs_r,
    px_s, px_r, pz_s, pz_r, ls_s, ls_r, ag_s, ag_r, x_s, x_r, y_s, y_r, z_s, z_r, f_s, f_r, hq_s, hq_r, hx_s, hx_r, near2, near4,
):
    me = lax.axis_index("dp")
    vo = lax.axis_index("vocab")
    y, c = me // 2, me % 2
    z, x = vo // NX, vo % NX

    def dp_dev(o, cx):
        return {"dp": ((y + o) % NY) * 2 + (c + cx) % 2, "vocab": vo}

    def x_dev(r):
        return {"dp": me, "vocab": z * NX + (x + r) % NX}

    def z_dev(zz):
        return {"dp": me, "vocab": zz * NX + x}

    def rc(src, dst, ssem, rsem, dev):
        return pltpu.make_async_remote_copy(
            src_ref=src, dst_ref=dst, send_sem=ssem, recv_sem=rsem, device_id=dev, device_id_type=MESH
        )

    waits = []

    def send(src, dst, ssem, rsem, dev):
        copy = rc(src, dst, ssem, rsem, dev)
        copy.start()
        waits.append(copy)

    def wait_recv(dst, ssem, rsem):
        rc(dst, dst, ssem, rsem, dp_dev(0, 1)).wait_recv()

    collects = z % 2 == c

    wcopies = []
    for q in range(NQ):
        rows = pl.ds(q * QC, QC)
        wcopies.append(pltpu.make_async_copy(weight.at[rows], wv.at[rows], w_sem.at[q]))
    own_h = pltpu.make_async_copy(hidden.at[:, pl.ds(pl.multiple_of(me * FEAT, FEAT), FEAT)], hv.at[0, 0], own_sem)
    own_h.start()
    id_copies = [
        pltpu.make_async_copy(ids_in, ids, id_sem.at[0]), pltpu.make_async_copy(logits_in, logits, id_sem.at[1])
    ]
    for w in id_copies + wcopies:
        w.start()

    barrier = pltpu.get_barrier_semaphore()

    def greet(dev):
        pl.semaphore_signal(barrier, inc=1, device_id=dev, device_id_type=MESH)

    for o in range(NY):
        for cx in range(NC):
            if o or cx:
                greet(dp_dev(o, cx))
    for r in range(1, NX):
        greet(x_dev(r))
    for r in (1, 2, NZ - 2, NZ - 1):
        greet(z_dev((z + r) % NZ))

    pl.semaphore_wait(barrier, 7 + (NX - 1) + 4)

    def tell(sem, step):
        for r in (step, NZ - step):
            pl.semaphore_signal(sem, inc=1, device_id=z_dev((z + r) % NZ), device_id_type=MESH)


    quarter = pl.ds(pl.multiple_of(x * 128, 128), 128)
    for cx in range(NC):
        dev = dp_dev(2, cx)
        cols = pl.ds(pl.multiple_of(dev["dp"] * FEAT + x * 128, 128), 128)
        send(hidden.at[:, cols], hv.at[2, cx, :, quarter], hq_s.at[cx], hq_r.at[cx], dev)
    for o, cx in ((1, 0), (3, 0), (1, 1), (3, 1), (0, 1)):
        dev = dp_dev(o, cx)
        back = (-o) % NY
        cols = pl.ds(pl.multiple_of(dev["dp"] * FEAT, FEAT), FEAT)
        send(hidden.at[:, cols], hv.at[back, cx], hs_sem.at[o, cx], hr_sem.at[back, cx], dev)
    tell(near2, 2)

    for w in id_copies:
        w.wait()
    lg = logits[...]
    logp = lg - jnp.log(jnp.sum(jnp.exp(lg), axis=1, keepdims=True))
    pr = jnp.exp(logp)
    prob[...] = pr
    entropy = jnp.sum(pr * logp, axis=1, keepdims=True)

    first = vo * VOCAB
    rows16 = lax.broadcasted_iota(jnp.int32, (NHI, K), 0)
    rows128 = lax.broadcasted_iota(jnp.int32, (128, K), 0)

    def target_tokens(n):
        for k in range(4):
            t = n * 4 + k
            place = ids[pl.ds(t, 1), :] - first
            p = prob[pl.ds(t, 1), :]
            a = jnp.where((place >> 7) == rows16, p, 0.0)
            a1 = a.astype(BF16)
            rest = a - a1.astype(F32)
            a2 = rest.astype(BF16)
            a3 = (rest - a2.astype(F32)).astype(BF16)
            b = jnp.where((place & 127) == rows128, 1.0, 0.0).astype(BF16)
            both = mm(jnp.concatenate([a1, a2, a3], axis=0), b, 1, 1)
            tgt[t] = both[0:NHI] + both[NHI:2 * NHI] + both[2 * NHI:3 * NHI]

    pl.loop(0, 5)(target_tokens)
    for cx in range(NC):
        part = hv.at[2, cx, :, quarter]
        wait_recv(part, hq_s.at[cx], hq_r.at[cx])
        for r in range(1, NX):
            send(part, part, hx_s.at[cx, r], hx_r.at[cx, (-r) % NX], x_dev(r))
    pl.loop(5, TOK // 4)(target_tokens)
    pl.semaphore_wait(near2, 2)
    tell(near4, 4)
    for q in range(NQ):
        wcopies[q].wait()
    def hidden_far(cx):
        for r in range(1, NX):
            part = hv.at[2, cx, :, pl.ds(pl.multiple_of(((x + r) % NX) * 128, 128), 128)]
            wait_recv(part, hx_s.at[cx, r], hx_r.at[cx, r])

    for o in (0, 1, 3):
        wait_recv(hv.at[o, 1], hs_sem.at[o, 1], hr_sem.at[o, 1])
    hidden_far(1)

    def q_of(s):
        return (s % 2) * 2 + s // 2

    def sib_copy(q):
        return rc(psib.at[q], srecv.at[q], ss_sem.at[q], sr_sem.at[q], dp_dev(0, 1))

    own_h.wait()
    for o in (1, 3):
        wait_recv(hv.at[o, 0], hs_sem.at[o, 0], hr_sem.at[o, 0])
    hidden_far(0)

    def way(q):
        return 1 + 2 * (q // 2)

    def opp_copy(q):
        return rc(enc_opp.at[q], in_opp.at[q], rs_s.at[0, q], rs_r.at[0, q], dp_dev(way(q), 0))

    def nb_copy(q, o):
        slot, back = o // 2, 1 - o // 2
        return rc(enc_nb.at[q, slot], in_nb.at[q, back], rs_s.at[1 + slot, q], rs_r.at[1 + back, q], dp_dev(o, 0))

    def logits_part(q, cx):
        hb = hv[:, cx].reshape(NY * TOK, FEAT)
        part = mm(hb, wv[pl.ds(pl.multiple_of(q * QC, QC), QC), :], 1, 1)
        return part.reshape(NY, TOK, QC)

    @pl.loop(0, NQ + 3)
    def _(s):
        @pl.when(s < NQ)
        def _():
            q = q_of(s)
            psib[q] = logits_part(q, 1)
            sib_copy(q).start()

        @pl.when(jnp.logical_and(s > 0, s <= NQ))
        def _():
            q = q_of(s - 1)
            pown[q] = logits_part(q, 0)
            wait_recv(srecv.at[q], ss_sem.at[q], sr_sem.at[q])
            enc_opp[q] = encode(pown[q, 2] + srecv[q, 2])
            opp_copy(q).start()
            other = 4 - way(q)
            enc_nb[q, other // 2] = encode(pown[q, other] + srecv[q, other])
            nb_copy(q, other).start()

        @pl.when(s > 2)
        def _():
            q = q_of(s - 3)
            wait_recv(in_opp.at[q], rs_s.at[0, q], rs_r.at[0, q])
            o = way(q)
            enc_nb[q, o // 2] = encode(pown[q, o] + srecv[q, o] + decode(in_opp[q]))
            nb_copy(q, o).start()

    tot = jnp.zeros((TOK, 128), F32)
    crs = jnp.zeros((TOK, 128), F32)
    for s in range(NQ):
        q = q_of(s)
        for slot in range(2):
            wait_recv(in_nb.at[q, slot], rs_s.at[1 + slot, q], rs_r.at[1 + slot, q])
        for k in range(QC // 128):
            cols = slice(k * 128, (k + 1) * 128)
            hi = q * (QC // 128) + k
            raw = (
                pown[q, 0, :, cols] + srecv[q, 0, :, cols]
                + decode(in_nb[q, 0, :, cols]) + decode(in_nb[q, 1, :, cols])
            )
            squash = jnp.tanh(raw * (1.0 / soft_cap))
            student = soft_cap * squash
            expo = jnp.exp(student)
            es[hi] = expo
            om[hi] = 1.0 - squash * squash
            tot = tot + expo
            crs = crs + tgt[:, hi, :] * student

    lane = lax.broadcasted_iota(jnp.int32, (TOK, 128), 1)
    row = lax.broadcasted_iota(jnp.int32, (TOK, 128), 0)
    mine = jnp.where(lane == row, jnp.sum(tot, axis=1, keepdims=True), 0.0) + jnp.where(
        lane == row + 64, jnp.sum(crs, axis=1, keepdims=True), 0.0
    )
    psx[x] = jnp.sum(mine, axis=0, keepdims=True)
    for r in range(1, NX):
        send(psx.at[x], psx.at[x], px_s.at[r], px_r.at[x], x_dev(r))
    for r in range(1, NX):
        src = (x + r) % NX
        wait_recv(psx.at[src], px_s.at[r], px_r.at[src])
    pl.semaphore_wait(near4, 2)
    psz[z] = psx[0] + psx[1] + psx[2] + psx[3]
    for r in range(1, NZ):
        send(psz.at[z], psz.at[z], pz_s.at[r], pz_r.at[z], z_dev((z + r) % NZ))
    for r in range(1, NZ):
        src = (z + r) % NZ
        wait_recv(psz.at[src], pz_s.at[r], pz_r.at[src])
    sums = psz[0]
    for k in range(1, NZ):
        sums = sums + psz[k]
    sums = jnp.broadcast_to(sums, (TOK, 128))
    total = jnp.sum(jnp.where(lane == row, sums, 0.0), axis=1, keepdims=True)
    cross = jnp.sum(jnp.where(lane == row + 64, sums, 0.0), axis=1, keepdims=True)
    inv = 1.0 / total
    for hi in range(NHI):
        g = (es[hi] * inv - tgt[:, hi, :]) * om[hi]
        gv[0, 0, :, hi * 128:(hi + 1) * 128] = g.astype(BF16)

    half = [pl.ds(0, VOCAB // 2), pl.ds(VOCAB // 2, VOCAB // 2)]

    def pass_on(n, o, h, do, dcx):
        back = (o - do) % NY
        src = gv.at[o, 0] if h is None else gv.at[o, 0, :, half[h]]
        dst = gv.at[back, dcx] if h is None else gv.at[back, dcx, :, half[h]]
        send(src, dst, ag_s.at[n], ag_r.at[n], dp_dev(do, dcx))

    def arrived(n, o, cx, h):
        dst = gv.at[o, cx] if h is None else gv.at[o, cx, :, half[h]]
        wait_recv(dst, ag_s.at[n], ag_r.at[n])

    pass_on(0, 0, 0, 1, 0)
    pass_on(1, 0, 1, 3, 0)
    pass_on(2, 0, None, 0, 1)
    pass_on(3, 0, 1, 1, 0)
    pass_on(4, 0, 0, 3, 0)

    token_loss = entropy - cross + jnp.log(total)
    lossb[me] = jnp.broadcast_to(jnp.sum(token_loss, axis=0, keepdims=True), (1, 128))
    for o in range(NY):
        for cx in range(NC):
            if o or cx:
                dev = dp_dev(o, cx)
                send(lossb.at[me], lossb.at[me], ls_s.at[o * 2 + cx], ls_r.at[me], dev)

    def terms(o):
        ga = gv[o].reshape(2 * TOK, VOCAB)
        part = [mm(ga, wv[:, n * 256:(n + 1) * 256], 1, 0) for n in range(2)]
        for m in range(NX):
            cols = slice(m * 64, (m + 1) * 64)
            piece = jnp.concatenate([part[0][:, cols], part[1][:, cols]], axis=1)
            gt[o, m] = piece
            xs[o, m] = piece.astype(BF16)
        for r in range(1, NX):
            there = (x + r) % NX
            send(xs.at[o, there], xr.at[o, (-r) % NX - 1], x_s.at[o, r - 1], x_r.at[o, (-r) % NX - 1], x_dev(r))

    def to_y(o):
        for r in range(NX - 1):
            wait_recv(xr.at[o, r], x_s.at[o, r], x_r.at[o, r])
        val = gt[o, x]
        for r in range(NX - 1):
            val = val + xr[o, r].astype(F32)
        for cx in range(NC):
            mine = val[cx * TOK:(cx + 1) * TOK].astype(BF16)
            if o or cx:
                ys[o, cx] = mine
                back = (-o) % NY
                send(ys.at[o, cx], yr.at[back, cx], y_s.at[o, cx], y_r.at[back, cx], dp_dev(o, cx))
            else:
                yr[0, 0] = mine

    zsends = []

    def to_z(o):
        for cx in range(NC):
            if o or cx:
                wait_recv(yr.at[o, cx], y_s.at[o, cx], y_r.at[o, cx])
            zd = 2 * dp_dev(o, cx)["dp"] + c
            r = (z - zd + NZ) % NZ
            copy = rc(yr.at[o, cx], zr.at[r], z_s.at[o, cx], z_r.at[r], z_dev(zd))

            @pl.when(r != 0)
            def _():
                copy.start()

            zsends.append((r, copy))

            @pl.when(r == 0)
            def _():
                zr[0] = yr[o, cx]

    arrived(0, 3, 0, 0)
    pass_on(5, 3, 0, 1, 0)
    pass_on(7, 3, 0, 0, 1)
    arrived(1, 1, 0, 1)
    pass_on(6, 1, 1, 3, 0)
    pass_on(8, 1, 1, 0, 1)
    arrived(2, 0, 1, None)
    terms(0)
    arrived(3, 3, 0, 1)
    pass_on(9, 3, 1, 0, 1)
    arrived(4, 1, 0, 0)
    pass_on(10, 1, 0, 0, 1)
    arrived(8, 1, 1, 1)
    arrived(10, 1, 1, 0)
    terms(1)
    arrived(7, 3, 1, 0)
    arrived(9, 3, 1, 1)
    terms(3)
    to_y(0)
    arrived(5, 2, 0, 0)
    pass_on(11, 2, 0, 0, 1)
    arrived(6, 2, 0, 1)
    pass_on(12, 2, 1, 0, 1)
    to_z(0)
    arrived(11, 2, 1, 0)
    arrived(12, 2, 1, 1)
    terms(2)
    to_y(1)
    to_y(3)

    HB = 256

    def head_part(low, high):
        @pl.loop(low, high)
        def _(n):
            rows = pl.ds(pl.multiple_of(n * HB, HB), HB)
            ga = gv[:, :, :, rows].reshape(8 * TOK, HB)
            hb = hv[...].reshape(8 * TOK, FEAT)
            out_head[rows, :] = mm(ga, hb, 0, 0).astype(BF16)

    nh = VOCAB // HB
    head_part(0, 2)
    to_y(2)
    to_z(3)
    to_z(1)
    head_part(2, 4)
    to_z(2)
    head_part(4, nh)
    for o in range(NY):
        for cx in range(NC):
            if o or cx:
                src = dp_dev(o, cx)["dp"]
                wait_recv(lossb.at[src], ls_s.at[o * 2 + cx], ls_r.at[src])
    loss = lossb[0]
    for k in range(1, 8):
        loss = loss + lossb[k]
    out_loss[...] = loss * (1.0 / (8 * TOK))


    def pair_copy():
        return rc(fin, fin_in, f_s, f_r, z_dev(z + 1 - 2 * (z % 2)))

    @pl.when(collects)
    def _():
        acc = zr[0].astype(F32)
        for r in range(1, NZ):
            wait_recv(zr.at[r], f_s, z_r.at[r])
            acc = acc + zr[r].astype(F32)
        fin[...] = acc.astype(BF16)
        pair_copy().start()
        fin_in[...] = fin[...]


    @pl.when(jnp.logical_not(collects))
    def _():
        wait_recv(fin_in, f_s, f_r)

    both = fin_in[...].astype(F32)
    out_hidden[...] = jnp.where(z % 2 == 0, both[:, :64], both[:, 64:]).astype(BF16)

    for copy in waits:
        copy.wait_send()

    @pl.loop(0, NQ)
    def _(q):
        sib_copy(q).wait_send()
        opp_copy(q).wait_send()
        nb_copy(q, 1).wait_send()
        nb_copy(q, 3).wait_send()

    for r, copy in zsends:
        @pl.when(r != 0)
        def _():
            copy.wait_send()

    @pl.when(collects)
    def _():
        pair_copy().wait_send()


def per_device(hidden, head_weight, teacher_ids, teacher_logits):
    vm = pltpu.VMEM
    dma = pltpu.SemaphoreType.DMA
    scratch = [
        vm((TOK, K), jnp.int32),
        vm((TOK, K), F32),
        vm((VOCAB, FEAT), BF16),
        vm((NY, NC, TOK, FEAT), BF16),
        vm((NQ, NY, TOK, QC), F32),
        vm((NQ, NY, TOK, QC), F32),
        vm((NQ, NY, TOK, QC), F32),
        vm((NQ, TOK, QC), jnp.int16),
        vm((NQ, 2, TOK, QC), jnp.int16),
        vm((NQ, TOK, QC), jnp.int16),
        vm((NQ, 2, TOK, QC), jnp.int16),
        vm((TOK, K), F32),
        vm((TOK, NHI, 128), F32),
        vm((NHI, TOK, 128), F32),
        vm((NHI, TOK, 128), F32),
        vm((NX, 1, 128), F32),
        vm((NZ, 1, 128), F32),
        vm((8, 1, 128), F32),
        vm((NY, NC, TOK, VOCAB), BF16),
        vm((NY, NX, 2 * TOK, 128), F32),
        vm((NY, NX, 2 * TOK, 128), BF16),
        vm((NY, NX - 1, 2 * TOK, 128), BF16),
        vm((NY, NC, TOK, 128), BF16),
        vm((NY, NC, TOK, 128), BF16),
        vm((NZ, TOK, 128), BF16),
        vm((TOK, 128), BF16),
        vm((TOK, 128), BF16),
        dma((2,)), dma((NQ,)), dma, dma((NY, NC)), dma((NY, NC)), dma((NQ,)), dma((NQ,)), dma((3, NQ)), dma((3, NQ)),
        dma((NX,)), dma((NX,)), dma((NZ,)), dma((NZ,)), dma((8,)), dma((8,)), dma((13,)), dma((13,)),
        dma((NY, NX - 1)), dma((NY, NX - 1)), dma((NY, NC)), dma((NY, NC)), dma((NY, NC)), dma((NZ,)), dma, dma,
        dma((NC,)), dma((NC,)), dma((NC, NX)), dma((NC, NX)),
        pltpu.SemaphoreType.REGULAR, pltpu.SemaphoreType.REGULAR,
    ]
    hbm = pl.BlockSpec(memory_space=pltpu.HBM)
    vmem = pl.BlockSpec(memory_space=pltpu.VMEM)
    hidden_grad, head_grad, loss = pl.pallas_call(
        kernel,
        out_shape=(
            pltpu.VMEM((TOK, D // 64), BF16),
            pltpu.VMEM((VOCAB, FEAT), BF16),
            pltpu.VMEM((1, 128), F32),
        ),
        in_specs=[hbm, hbm, hbm, hbm],
        out_specs=(vmem, vmem, vmem),
        scratch_shapes=scratch,
        compiler_params=pltpu.CompilerParams(
            collective_id=0, has_side_effects=True, vmem_limit_bytes=56 * 1024 * 1024
        ),
    )(hidden, head_weight, teacher_ids, teacher_logits)
    return hidden_grad, head_grad, loss[0, 0]


def solution(mesh):
    in_specs = (P("dp", None), P("vocab", "dp"), P("dp", None), P("dp", None))
    out_specs = (P("dp", "vocab"), P("vocab", "dp"), P())
    return jax.shard_map(
        per_device, mesh=mesh, in_specs=in_specs, out_specs=out_specs, check_vma=False
    )
```

```python
import jax
import jax.numpy as jnp
from jax import lax
from jax.experimental import pallas as pl
from jax.experimental.pallas import tpu as pltpu
from jax.sharding import PartitionSpec as P

MESH = pl.DeviceIdType.MESH
F32 = jnp.float32
BF16 = jnp.bfloat16
soft_cap = 30.0

NY, NC, NX, NZ = 4, 2, 4, 16
TOK, D, K = 48, 4096, 256
FEAT = D // 8
VOCAB = 131072 // 64
NQ = 4
QC = VOCAB // NQ
NHI = VOCAB // 128
BEND = 48.0
LEVELS = 32767.0


def encode(x):
    return jnp.round(x * (LEVELS / (jnp.abs(x) + BEND))).astype(jnp.int32).astype(jnp.int16)


def decode(q):
    u = q.astype(jnp.int32).astype(F32)
    return u * (BEND / (LEVELS - jnp.abs(u)))


def mm(a, b, ca, cb):
    return lax.dot_general(a, b, (((ca,), (cb,)), ((), ())), preferred_element_type=F32)


def kernel(
    hidden, weight, ids_in, logits_in, out_hidden, out_head, out_loss,
    ids, logits, wv, hv, psib, pown, srecv, enc_opp, enc_nb, in_opp, in_nb,
    prob, tgt, es, om, psx, psz, lossb, gv, gt, xs, xr, ys, yr, zr, head, hidden_v, loss_v,
    id_sem, w_sem, own_sem, hs_sem, hr_sem, ss_sem, sr_sem, rs_s, rs_opp, rs_nb,
    px_s, px_r, pz_s, pz_r, ls_s, ls_r, ag_s, ag_r, x_s, x_r, y_s, y_r, z_s, z_r, head_sem, out_sem, near2, near4,
):
    me = lax.axis_index("dp")
    vo = lax.axis_index("vocab")
    y, c = me // 2, me % 2
    z, x = vo // NX, vo % NX

    def dp_dev(o, cx):
        return {"dp": ((y + o) % NY) * 2 + (c + cx) % 2, "vocab": vo}

    def x_dev(r):
        return {"dp": me, "vocab": z * NX + (x + r) % NX}

    def z_dev(zz):
        return {"dp": me, "vocab": zz * NX + x}

    def rc(src, dst, ssem, rsem, dev):
        return pltpu.make_async_remote_copy(
            src_ref=src, dst_ref=dst, send_sem=ssem, recv_sem=rsem, device_id=dev, device_id_type=MESH
        )


    def came(ref, sem):
        rc(ref, ref, hs_sem.at[0], sem, dp_dev(0, 1)).wait_recv()

    def gone(ref, sem):
        rc(ref, ref, sem, hr_sem.at[0], dp_dev(0, 1)).wait_send()

    w_copy = pltpu.make_async_copy(weight, wv, w_sem)
    own_h = pltpu.make_async_copy(hidden.at[:, pl.ds(pl.multiple_of(me * FEAT, FEAT), FEAT)], hv.at[0, 0], own_sem)
    own_h.start()
    id_copies = [
        pltpu.make_async_copy(ids_in, ids, id_sem.at[0]), pltpu.make_async_copy(logits_in, logits, id_sem.at[1])
    ]
    for w in id_copies:
        w.start()
    w_copy.start()

    barrier = pltpu.get_barrier_semaphore()

    def greet(dev):
        pl.semaphore_signal(barrier, inc=1, device_id=dev, device_id_type=MESH)

    for o in range(NY):
        for cx in range(NC):
            if o or cx:
                greet(dp_dev(o, cx))
    for r in range(1, NX):
        greet(x_dev(r))
    for r in (1, 2, NZ - 2, NZ - 1):
        greet(z_dev((z + r) % NZ))

    pl.semaphore_wait(barrier, 7 + (NX - 1) + 4)

    def tell(sem, step):
        for r in (step, NZ - step):
            pl.semaphore_signal(sem, inc=1, device_id=z_dev((z + r) % NZ), device_id_type=MESH)


    def hidden_copy(o, cx):
        dev = dp_dev(o, cx)
        back = (-o) % NY
        cols = pl.ds(pl.multiple_of(dev["dp"] * FEAT, FEAT), FEAT)
        n = (0, 1, 2, 1)[o]
        return rc(hidden.at[:, cols], hv.at[back, cx], hs_sem.at[n], hr_sem.at[n], dev)

    for o, cx in ((2, 0), (2, 1), (0, 1)):
        hidden_copy(o, cx).start()
    tell(near2, 2)

    for w in id_copies:
        w.wait()
    lg = logits[...]
    logp = lg - jnp.log(jnp.sum(jnp.exp(lg), axis=1, keepdims=True))
    pr = jnp.exp(logp)
    prob[...] = pr
    entropy = jnp.sum(pr * logp, axis=1, keepdims=True)

    first = vo * VOCAB
    rows16 = lax.broadcasted_iota(jnp.int32, (NHI, K), 0)
    rows128 = lax.broadcasted_iota(jnp.int32, (128, K), 0)

    def target_tokens(n):
        for k in range(4):
            t = n * 4 + k
            place = ids[pl.ds(t, 1), :] - first
            p = prob[pl.ds(t, 1), :]
            a = jnp.where((place >> 7) == rows16, p, 0.0)
            a1 = a.astype(BF16)
            rest = a - a1.astype(F32)
            a2 = rest.astype(BF16)
            a3 = (rest - a2.astype(F32)).astype(BF16)
            b = jnp.where((place & 127) == rows128, 1.0, 0.0).astype(BF16)
            both = mm(jnp.concatenate([a1, a2, a3], axis=0), b, 1, 1)
            tgt[t] = both[0:NHI] + both[NHI:2 * NHI] + both[2 * NHI:3 * NHI]


    place_of = (0, 2, 1, 3)

    def partial_logits(q, offsets):
        hb = jnp.concatenate([hv[o].reshape(NC * TOK, FEAT) for o in offsets], axis=0)
        part = mm(hb, wv[pl.ds(pl.multiple_of(q * QC, QC), QC), :], 1, 1)
        for n, o in enumerate(offsets):
            pown[q, place_of[o]] = part[2 * n * TOK:(2 * n + 1) * TOK]
            psib[q, place_of[o]] = part[(2 * n + 1) * TOK:(2 * n + 2) * TOK]

    def sib_copy(q, offsets):
        places = pl.ds(place_of[offsets[0]], len(offsets))
        n = 0 if offsets == (0,) else 1 + q + NQ * (len(offsets) - 1)
        return rc(psib.at[q, places], srecv.at[q, places], ss_sem, sr_sem.at[n], dp_dev(0, 1))

    def q_of(s):
        return (s % 2) * 2 + s // 2

    def way(q):
        return 1 + 2 * (q // 2)

    def opp_copy(q):
        return rc(enc_opp.at[q], in_opp.at[q], rs_s.at[0], rs_opp.at[q], dp_dev(way(q), 0))

    def nb_copy(q, o):
        slot, back = o // 2, 1 - o // 2
        return rc(enc_nb.at[q, slot], in_nb.at[q, back], rs_s.at[1], rs_nb.at[q], dp_dev(o, 0))

    w_copy.wait()
    own_h.wait()
    came(hv.at[0, 1], hr_sem.at[0])

    @pl.loop(0, NQ)
    def _(q):
        partial_logits(q, (0,))
        sib_copy(q, (0,)).start()

    gone(hv.at[0], hs_sem.at[2])
    for o, cx in ((1, 0), (3, 0), (1, 1), (3, 1)):
        hidden_copy(o, cx).start()
    pl.loop(0, TOK // 4)(target_tokens)
    pl.semaphore_wait(near2, 2)
    tell(near4, 4)
    came(hv.at[2], hr_sem.at[2])

    @pl.loop(0, NQ + 1)
    def _(s):
        @pl.when(s < NQ)
        def _():
            q = q_of(s)
            partial_logits(q, (2,))
            sib_copy(q, (2,)).start()

        @pl.when(s > 0)
        def _():
            q = q_of(s - 1)
            sib_copy(q, (2,)).wait_recv()
            enc_opp[q] = encode(pown[q, 1] + srecv[q, 1])
            opp_copy(q).start()

    came(hv.at[pl.ds(0, 2)], hr_sem.at[1])

    @pl.loop(0, NQ + 2)
    def _(s):
        @pl.when(s < NQ)
        def _():
            q = q_of(s)
            partial_logits(q, (1, 3))
            sib_copy(q, (1, 3)).start()

        @pl.when(jnp.logical_and(s > 0, s <= NQ))
        def _():
            q = q_of(s - 1)
            sib_copy(q, (1, 3)).wait_recv()
            o = 4 - way(q)
            enc_nb[q, o // 2] = encode(pown[q, 2 + o // 2] + srecv[q, 2 + o // 2])
            nb_copy(q, o).start()

        @pl.when(s > 1)
        def _():
            q = q_of(s - 2)
            opp_copy(q).wait_recv()
            o = way(q)
            enc_nb[q, o // 2] = encode(pown[q, 2 + o // 2] + srecv[q, 2 + o // 2] + decode(in_opp[q]))
            nb_copy(q, o).start()

    tot = jnp.zeros((TOK, 128), F32)
    crs = jnp.zeros((TOK, 128), F32)
    came(srecv.at[:, 0], sr_sem.at[0])
    for s in range(NQ):
        q = q_of(s)
        came(in_nb.at[q], rs_nb.at[q])
        for k in range(QC // 128):
            cols = slice(k * 128, (k + 1) * 128)
            hi = q * (QC // 128) + k
            raw = (
                pown[q, 0, :, cols] + srecv[q, 0, :, cols]
                + decode(in_nb[q, 0, :, cols]) + decode(in_nb[q, 1, :, cols])
            )
            squash = jnp.tanh(raw * (1.0 / soft_cap))
            student = soft_cap * squash
            expo = jnp.exp(student)
            es[hi] = expo
            om[hi] = 1.0 - squash * squash
            tot = tot + expo
            crs = crs + tgt[:, hi, :] * student

    lane = lax.broadcasted_iota(jnp.int32, (TOK, 128), 1)
    row = lax.broadcasted_iota(jnp.int32, (TOK, 128), 0)
    mine = jnp.where(lane == row, jnp.sum(tot, axis=1, keepdims=True), 0.0) + jnp.where(
        lane == row + 64, jnp.sum(crs, axis=1, keepdims=True), 0.0
    )
    psx[x] = jnp.sum(mine, axis=0, keepdims=True)
    for r in range(1, NX):
        rc(psx.at[x], psx.at[x], px_s, px_r, x_dev(r)).start()
    came(psx.at[pl.ds(0, NX - 1)], px_r)
    pl.semaphore_wait(near4, 2)
    psz[z] = psx[0] + psx[1] + psx[2] + psx[3]
    for r in (8, 7, 9, 6, 10, 5, 11, 4, 12, 3, 13, 2, 14, 1, 15):
        rc(psz.at[z], psz.at[z], pz_s, pz_r, z_dev((z + r) % NZ)).start()
    came(psz.at[pl.ds(0, NZ - 1)], pz_r)
    sums = psz[0]
    for k in range(1, NZ):
        sums = sums + psz[k]
    sums = jnp.broadcast_to(sums, (TOK, 128))
    total = jnp.sum(jnp.where(lane == row, sums, 0.0), axis=1, keepdims=True)
    cross = jnp.sum(jnp.where(lane == row + 64, sums, 0.0), axis=1, keepdims=True)
    inv = 1.0 / total
    for hi in range(NHI):
        g = (es[hi] * inv - tgt[:, hi, :]) * om[hi]
        gv[0, 0, :, hi * 128:(hi + 1) * 128] = g.astype(BF16)

    half = [pl.ds(0, VOCAB // 2), pl.ds(VOCAB // 2, VOCAB // 2)]

    def pass_on(o, h, do, dcx, ssem, rsem):
        back = (o - do) % NY
        src = gv.at[o, 0] if h is None else gv.at[o, 0, :, half[h]]
        dst = gv.at[back, dcx] if h is None else gv.at[back, dcx, :, half[h]]
        rc(src, dst, ag_s.at[ssem], ag_r.at[rsem], dp_dev(do, dcx)).start()

    pass_on(0, 0, 1, 0, 0, 0)
    pass_on(0, 1, 3, 0, 0, 1)
    pass_on(0, None, 0, 1, 1, 2)

    token_loss = entropy - cross + jnp.log(total)
    lossb[me] = jnp.broadcast_to(jnp.sum(token_loss, axis=0, keepdims=True), (1, 128))
    for o in range(NY):
        for cx in range(NC):
            if o or cx:
                dev = dp_dev(o, cx)
                rc(lossb.at[me], lossb.at[me], ls_s, ls_r, dev).start()

    def terms(offsets):
        ga = jnp.concatenate([gv[o].reshape(NC * TOK, VOCAB) for o in offsets], axis=0)
        part = [mm(ga, wv[:, n * 256:(n + 1) * 256], 1, 0) for n in range(2)]
        for n, o in enumerate(offsets):
            rows = slice(n * NC * TOK, (n + 1) * NC * TOK)
            for m in range(NX):
                cols = slice(m * 64, (m + 1) * 64)
                piece = jnp.concatenate([part[0][rows, cols], part[1][rows, cols]], axis=1)
                gt[o, m] = piece
                xs[o, m] = piece.astype(BF16)
            for r in range(1, NX):
                there = (x + r) % NX
                rc(xs.at[o, there], xr.at[o, (-r) % NX - 1], x_s, x_r.at[o], x_dev(r)).start()

    def to_y(o):
        came(xr.at[o], x_r.at[o])
        val = gt[o, x]
        for r in range(NX - 1):
            val = val + xr[o, r].astype(F32)
        for cx in range(NC):
            top, low = val[cx * TOK:cx * TOK + 24], val[cx * TOK + 24:(cx + 1) * TOK]
            gap = jnp.zeros((8, 128), F32)
            mine = jnp.concatenate(
                [
                    jnp.concatenate([top[:, :64], low[:, :64]], axis=1), gap,
                    jnp.concatenate([top[:, 64:], low[:, 64:]], axis=1), gap,
                ],
                axis=0,
            ).astype(BF16)
            if o or cx:
                n = o * NC + cx
                ys[n] = mine
                back = (-o) % NY
                rc(ys.at[n], yr.at[back, cx], y_s, y_r.at[back], dp_dev(o, cx)).start()
            else:
                yr[0, 0] = mine

    def to_z(o):
        came(yr.at[o] if o else yr.at[0, 1], y_r.at[o])
        for cx in range(NC):
            for h in range(2):
                zd = 2 * dp_dev(o, cx)["dp"] + h
                r = (z - zd + NZ) % NZ
                part = yr.at[o, cx, pl.ds(32 * h, 32)]
                copy = rc(part, zr.at[r], z_s, z_r, z_dev(zd))
                here = r == 0

                @pl.when(jnp.logical_not(here))
                def _():
                    copy.start()

                @pl.when(here)
                def _():
                    zr[0] = yr[o, cx, 32 * h:32 * h + 32]

    gone(gv.at[0, 0], ag_s.at[0])
    pass_on(0, 1, 1, 0, 2, 3)
    pass_on(0, 0, 3, 0, 2, 3)
    came(gv.at[3, 0, :, half[0]], ag_r.at[0])
    pass_on(3, 0, 1, 0, 3, 4)
    pass_on(3, 0, 0, 1, 4, 6)
    came(gv.at[1, 0, :, half[1]], ag_r.at[1])
    pass_on(1, 1, 3, 0, 3, 5)
    pass_on(1, 1, 0, 1, 4, 6)
    came(gv.at[0, 1], ag_r.at[2])
    terms((0,))
    came(gv.at[0, 0], ag_r.at[3])
    pass_on(3, 1, 0, 1, 4, 6)
    pass_on(1, 0, 0, 1, 4, 6)
    came(gv.at[0], ag_r.at[6])
    terms((1, 3))
    for h in range(2):
        came(gv.at[2, 0, :, half[h]], ag_r.at[4 + h])
        pass_on(2, h, 0, 1, 5, 7)
    to_y(0)
    came(gv.at[2, 1], ag_r.at[7])
    terms((2,))
    to_z(0)
    to_y(1)
    to_y(3)

    HB = 256

    def head_copy(n):
        rows = pl.ds(pl.multiple_of(n * HB, HB), HB)
        return pltpu.make_async_copy(head.at[rows], out_head.at[rows], head_sem)

    def head_part(low, high):
        @pl.loop(low, high)
        def _(n):
            rows = pl.ds(pl.multiple_of(n * HB, HB), HB)
            ga = gv[:, :, :, rows].reshape(8 * TOK, HB)
            hb = hv[...].reshape(8 * TOK, FEAT)
            head[rows, :] = mm(ga, hb, 0, 0).astype(BF16)
            head_copy(n).start()

    nh = VOCAB // HB
    head_part(0, 2)
    to_y(2)
    to_z(3)
    to_z(1)
    head_part(2, 4)
    to_z(2)
    head_part(4, nh)
    came(lossb.at[pl.ds(0, 7)], ls_r)
    loss = lossb[0]
    for k in range(1, 8):
        loss = loss + lossb[k]
    loss_v[...] = loss * (1.0 / (8 * TOK))
    loss_copy = pltpu.make_async_copy(loss_v, out_loss, out_sem.at[0])
    loss_copy.start()


    acc = zr[0].astype(F32)
    came(zr.at[pl.ds(1, NZ - 1)], z_r)
    for r in range(1, NZ):
        acc = acc + zr[r].astype(F32)
    hidden_v[...] = jnp.concatenate([acc[0:24, :64], acc[0:24, 64:]], axis=0).astype(BF16)
    hidden_out = pltpu.make_async_copy(hidden_v, out_hidden, out_sem.at[1])
    hidden_out.start()

    gone(hv.at[0, 1], hs_sem.at[0])
    gone(hv.at[pl.ds(0, 2)], hs_sem.at[1])
    gone(psib, ss_sem)
    gone(enc_opp, rs_s.at[0])
    gone(enc_nb, rs_s.at[1])
    gone(psx.at[pl.ds(0, NX - 1)], px_s)
    gone(psz.at[pl.ds(0, NZ - 1)], pz_s)
    gone(lossb.at[pl.ds(0, 7)], ls_s)
    gone(gv.at[0, 0], ag_s.at[1])
    gone(gv.at[0, 0], ag_s.at[2])
    gone(gv.at[0, 0], ag_s.at[3])
    gone(gv.at[0], ag_s.at[4])
    gone(gv.at[0, 0], ag_s.at[5])
    gone(xr, x_s)
    gone(ys.at[pl.ds(1, 7)], y_s)
    gone(zr.at[pl.ds(1, NZ - 1)], z_s)
    pltpu.make_async_copy(head, out_head, head_sem).wait()
    loss_copy.wait()
    hidden_out.wait()


def per_device(hidden, head_weight, teacher_ids, teacher_logits):
    vm = pltpu.VMEM
    dma = pltpu.SemaphoreType.DMA
    scratch = [
        vm((TOK, K), jnp.int32),
        vm((TOK, K), F32),
        vm((VOCAB, FEAT), BF16),
        vm((NY, NC, TOK, FEAT), BF16),
        vm((NQ, NY, TOK, QC), F32),
        vm((NQ, NY, TOK, QC), F32),
        vm((NQ, NY, TOK, QC), F32),
        vm((NQ, TOK, QC), jnp.int16),
        vm((NQ, 2, TOK, QC), jnp.int16),
        vm((NQ, TOK, QC), jnp.int16),
        vm((NQ, 2, TOK, QC), jnp.int16),
        vm((TOK, K), F32),
        vm((TOK, NHI, 128), F32),
        vm((NHI, TOK, 128), F32),
        vm((NHI, TOK, 128), F32),
        vm((NX, 1, 128), F32),
        vm((NZ, 1, 128), F32),
        vm((8, 1, 128), F32),
        vm((NY, NC, TOK, VOCAB), BF16),
        vm((NY, NX, 2 * TOK, 128), F32),
        vm((NY, NX, 2 * TOK, 128), BF16),
        vm((NY, NX - 1, 2 * TOK, 128), BF16),
        vm((NY * NC, 64, 128), BF16),
        vm((NY, NC, 64, 128), BF16),
        vm((NZ, 32, 128), BF16),
        vm((VOCAB, FEAT), BF16),
        vm((TOK, D // 64), BF16),
        vm((1, 128), F32),
        dma((2,)), dma, dma, dma((3,)), dma((3,)), dma, dma((1 + 2 * NQ,)), dma((2,)), dma((NQ,)), dma((NQ,)),
        dma, dma, dma, dma, dma, dma, dma((6,)), dma((8,)), dma, dma((NY,)), dma, dma((NY,)), dma, dma, dma, dma((2,)),
        pltpu.SemaphoreType.REGULAR, pltpu.SemaphoreType.REGULAR,
    ]
    hbm = pl.BlockSpec(memory_space=pltpu.HBM)
    anys = pl.BlockSpec(memory_space=pl.ANY)
    hidden_grad, head_grad, loss = pl.pallas_call(
        kernel,
        out_shape=(
            pltpu.VMEM((TOK, D // 64), BF16),
            pltpu.VMEM((VOCAB, FEAT), BF16),
            pltpu.VMEM((1, 128), F32),
        ),
        in_specs=[hbm, hbm, hbm, hbm],
        out_specs=(anys, anys, anys),
        scratch_shapes=scratch,
        compiler_params=pltpu.CompilerParams(
            collective_id=0, has_side_effects=True, vmem_limit_bytes=56 * 1024 * 1024
        ),
    )(hidden, head_weight, teacher_ids, teacher_logits)
    return hidden_grad, head_grad, loss[0, 0]


def solution(mesh):
    in_specs = (P("dp", None), P("vocab", "dp"), P("dp", None), P("dp", None))
    out_specs = (P("dp", "vocab"), P("vocab", "dp"), P())
    return jax.shard_map(
        per_device, mesh=mesh, in_specs=in_specs, out_specs=out_specs, check_vma=False
    )
```

```python
import jax
import jax.numpy as jnp
from jax import lax
from jax.experimental import pallas as pl
from jax.experimental.pallas import tpu as pltpu
from jax.sharding import PartitionSpec as P

MESH = pl.DeviceIdType.MESH
F32 = jnp.float32
BF16 = jnp.bfloat16
soft_cap = 30.0

NY, NC, NX, NZ = 4, 2, 4, 16
TOK, D, K = 48, 4096, 256
FEAT = D // 8
VOCAB = 131072 // 64
NQ = 4
QC = VOCAB // NQ
NHI = VOCAB // 128
BEND = 48.0
LEVELS = 32767.0


def encode(x):
    return jnp.round(x * (LEVELS / (jnp.abs(x) + BEND))).astype(jnp.int32).astype(jnp.int16)


def decode(q):
    u = q.astype(jnp.int32).astype(F32)
    return u * (BEND / (LEVELS - jnp.abs(u)))


def mm(a, b, ca, cb):
    return lax.dot_general(a, b, (((ca,), (cb,)), ((), ())), preferred_element_type=F32)


def kernel(
    hidden, weight, ids_in, logits_in, out_hidden, out_head, out_loss,
    ids, logits, wv, hv, psib, pown, srecv, enc_opp, enc_nb, in_opp, in_nb,
    prob, tgt, es, om, psz, lossb, gv, xs, xr, zs, zr, head, hidden_v, loss_v,
    id_sem, w_sem, own_sem, hs_sem, hr_sem, ss_sem, sr_sem, rs_s, rs_opp, rs_nb,
    pz_s, pz_r, ls_s, ls_r, ag_s, ag_r, x_s, x_r, z_s, z_r, head_sem, out_sem, near2, near4, near8,
):
    me = lax.axis_index("dp")
    vo = lax.axis_index("vocab")
    y, c = me // 2, me % 2
    z, x = vo // NX, vo % NX

    def dp_dev(o, cx):
        return {"dp": ((y + o) % NY) * 2 + (c + cx) % 2, "vocab": vo}

    def x_dev(r):
        return {"dp": me, "vocab": z * NX + (x + r) % NX}

    def z_dev(zz):
        return {"dp": me, "vocab": zz * NX + x}

    def rc(src, dst, ssem, rsem, dev):
        return pltpu.make_async_remote_copy(
            src_ref=src, dst_ref=dst, send_sem=ssem, recv_sem=rsem, device_id=dev, device_id_type=MESH
        )


    def came(ref, sem):
        rc(ref, ref, hs_sem.at[0], sem, dp_dev(0, 1)).wait_recv()

    def gone(ref, sem):
        rc(ref, ref, sem, hr_sem.at[0], dp_dev(0, 1)).wait_send()

    barrier = pltpu.get_barrier_semaphore()

    def greet(dev):
        pl.semaphore_signal(barrier, inc=1, device_id=dev, device_id_type=MESH)

    for o in range(NY):
        for cx in range(NC):
            if o or cx:
                greet(dp_dev(o, cx))
    for r in range(1, NX):
        greet(x_dev(r))
    for r in (1, 2, NZ - 2, NZ - 1):
        greet(z_dev((z + r) % NZ))

    w_copy = pltpu.make_async_copy(weight, wv, w_sem)
    own_h = pltpu.make_async_copy(hidden.at[:, pl.ds(pl.multiple_of(me * FEAT, FEAT), FEAT)], hv.at[0, 0], own_sem)
    own_h.start()
    id_copies = [
        pltpu.make_async_copy(ids_in, ids, id_sem.at[0]), pltpu.make_async_copy(logits_in, logits, id_sem.at[1])
    ]
    for w in id_copies:
        w.start()
    w_copy.start()

    pl.semaphore_wait(barrier, 7 + (NX - 1) + 4)

    def tell(sem, *steps):
        for step in steps:
            for r in (step, NZ - step):
                pl.semaphore_signal(sem, inc=1, device_id=z_dev((z + r) % NZ), device_id_type=MESH)


    def hidden_copy(o, cx):
        dev = dp_dev(o, cx)
        back = (-o) % NY
        cols = pl.ds(pl.multiple_of(dev["dp"] * FEAT, FEAT), FEAT)
        n = (0, 1, 2, 1)[o]
        return rc(hidden.at[:, cols], hv.at[back, cx], hs_sem.at[n], hr_sem.at[n], dev)

    for o, cx in ((2, 0), (2, 1), (0, 1)):
        hidden_copy(o, cx).start()
    tell(near2, 1, 2)
    for r in range(1, NX):
        pl.semaphore_signal(near2, inc=1, device_id=x_dev(r), device_id_type=MESH)

    for w in id_copies:
        w.wait()
    lg = logits[...]
    logp = lg - jnp.log(jnp.sum(jnp.exp(lg), axis=1, keepdims=True))
    pr = jnp.exp(logp)
    prob[...] = pr
    entropy = jnp.sum(pr * logp, axis=1, keepdims=True)

    first = vo * VOCAB
    rows16 = lax.broadcasted_iota(jnp.int32, (NHI, K), 0)
    rows128 = lax.broadcasted_iota(jnp.int32, (128, K), 0)

    def target_tokens(n):
        for k in range(4):
            t = n * 4 + k
            place = ids[pl.ds(t, 1), :] - first
            p = prob[pl.ds(t, 1), :]
            a = jnp.where((place >> 7) == rows16, p, 0.0)
            a1 = a.astype(BF16)
            rest = a - a1.astype(F32)
            a2 = rest.astype(BF16)
            a3 = (rest - a2.astype(F32)).astype(BF16)
            b = jnp.where((place & 127) == rows128, 1.0, 0.0).astype(BF16)
            both = mm(jnp.concatenate([a1, a2, a3], axis=0), b, 1, 1)
            tgt[t] = both[0:NHI] + both[NHI:2 * NHI] + both[2 * NHI:3 * NHI]

    pl.loop(0, 8)(target_tokens)
    gone(hv.at[0], hs_sem.at[2])
    for o, cx in ((1, 0), (3, 0), (1, 1), (3, 1)):
        hidden_copy(o, cx).start()

    place_of = (0, 2, 1, 3)

    def partial_logits(q, offsets):
        hb = jnp.concatenate([hv[o].reshape(NC * TOK, FEAT) for o in offsets], axis=0)
        part = mm(hb, wv[pl.ds(pl.multiple_of(q * QC, QC), QC), :], 1, 1)
        for n, o in enumerate(offsets):
            pown[q, place_of[o]] = part[2 * n * TOK:(2 * n + 1) * TOK]
            psib[q, place_of[o]] = part[(2 * n + 1) * TOK:(2 * n + 2) * TOK]

    def sib_copy(q, offsets):
        places = pl.ds(place_of[offsets[0]], len(offsets))
        n = 0 if offsets == (0,) else 1 + q + NQ * (len(offsets) - 1)
        return rc(psib.at[q, places], srecv.at[q, places], ss_sem, sr_sem.at[n], dp_dev(0, 1))

    def q_of(s):
        return (s % 2) * 2 + s // 2

    def way(q):
        return 1 + 2 * (q // 2)

    def opp_copy(q):
        return rc(enc_opp.at[q], in_opp.at[q], rs_s.at[0], rs_opp.at[q], dp_dev(way(q), 0))

    def nb_copy(q, o):
        slot, back = o // 2, 1 - o // 2
        return rc(enc_nb.at[q, slot], in_nb.at[q, back], rs_s.at[1], rs_nb.at[q], dp_dev(o, 0))

    w_copy.wait()
    own_h.wait()
    came(hv.at[0, 1], hr_sem.at[0])

    @pl.loop(0, NQ)
    def _(q):
        partial_logits(q, (0,))
        sib_copy(q, (0,)).start()

    pl.loop(8, TOK // 4)(target_tokens)
    pl.semaphore_wait(near2, 4 + NX - 1)
    tell(near4, 4)
    came(hv.at[2], hr_sem.at[2])

    @pl.loop(0, NQ)
    def _(s):
        q = q_of(s)
        partial_logits(q, (2,))
        sib_copy(q, (2,)).start()

    came(hv.at[pl.ds(0, 2)], hr_sem.at[1])

    @pl.loop(0, NQ + 4)
    def _(s):
        @pl.when(s < NQ)
        def _():
            q = q_of(s)
            sib_copy(q, (2,)).wait_recv()
            enc_opp[q] = encode(pown[q, 1] + srecv[q, 1])
            opp_copy(q).start()
            partial_logits(q, (1, 3))
            sib_copy(q, (1, 3)).start()

        @pl.when(jnp.logical_and(s > 1, s <= NQ + 1))
        def _():
            q = q_of(s - 2)
            sib_copy(q, (1, 3)).wait_recv()
            o = 4 - way(q)
            enc_nb[q, o // 2] = encode(pown[q, 2 + o // 2] + srecv[q, 2 + o // 2])
            nb_copy(q, o).start()

        @pl.when(s > 3)
        def _():
            q = q_of(s - 4)
            opp_copy(q).wait_recv()
            o = way(q)
            enc_nb[q, o // 2] = encode(pown[q, 2 + o // 2] + srecv[q, 2 + o // 2] + decode(in_opp[q]))
            nb_copy(q, o).start()

    pl.semaphore_wait(near4, 2)
    tell(near8, 4)
    tot = jnp.zeros((TOK, 128), F32)
    crs = jnp.zeros((TOK, 128), F32)
    came(srecv.at[:, 0], sr_sem.at[0])
    for s in range(NQ):
        q = q_of(s)
        came(in_nb.at[q], rs_nb.at[q])
        for k in range(QC // 128):
            cols = slice(k * 128, (k + 1) * 128)
            hi = q * (QC // 128) + k
            raw = (
                pown[q, 0, :, cols] + srecv[q, 0, :, cols]
                + decode(in_nb[q, 0, :, cols]) + decode(in_nb[q, 1, :, cols])
            )
            squash = jnp.tanh(raw * (1.0 / soft_cap))
            student = soft_cap * squash
            expo = jnp.exp(student)
            es[hi] = expo
            om[hi] = 1.0 - squash * squash
            tot = tot + expo
            crs = crs + tgt[:, hi, :] * student

    lane = lax.broadcasted_iota(jnp.int32, (TOK, 128), 1)
    row = lax.broadcasted_iota(jnp.int32, (TOK, 128), 0)
    mine = jnp.where(lane == row, jnp.sum(tot, axis=1, keepdims=True), 0.0) + jnp.where(
        lane == row + 64, jnp.sum(crs, axis=1, keepdims=True), 0.0
    )
    psz[vo] = jnp.sum(mine, axis=0, keepdims=True)
    pl.semaphore_wait(near8, 2)

    @pl.loop(0, NZ * NX - 1)
    def _(n):
        there = (vo + 1 + (n + NZ * NX // 2 - 1) % (NZ * NX - 1)) % (NZ * NX)
        rc(psz.at[vo], psz.at[vo], pz_s, pz_r, {"dp": me, "vocab": there}).start()

    came(psz.at[pl.ds(0, NZ * NX - 1)], pz_r)
    sums = jnp.sum(psz[...], axis=0)
    sums = jnp.broadcast_to(sums, (TOK, 128))
    total = jnp.sum(jnp.where(lane == row, sums, 0.0), axis=1, keepdims=True)
    cross = jnp.sum(jnp.where(lane == row + 64, sums, 0.0), axis=1, keepdims=True)
    inv = 1.0 / total
    for hi in range(NHI):
        g = (es[hi] * inv - tgt[:, hi, :]) * om[hi]
        gv[0, 0, :, hi * 128:(hi + 1) * 128] = g.astype(BF16)

    half = [pl.ds(0, VOCAB // 2), pl.ds(VOCAB // 2, VOCAB // 2)]

    def pass_on(o, h, do, dcx, ssem, rsem):
        back = (o - do) % NY
        src = gv.at[o, 0] if h is None else gv.at[o, 0, :, half[h]]
        dst = gv.at[back, dcx] if h is None else gv.at[back, dcx, :, half[h]]
        rc(src, dst, ag_s.at[ssem], ag_r.at[rsem], dp_dev(do, dcx)).start()

    pass_on(0, 0, 1, 0, 0, 0)
    pass_on(0, 1, 3, 0, 0, 1)
    pass_on(0, None, 0, 1, 1, 2)

    token_loss = entropy - cross + jnp.log(total)
    lossb[me] = jnp.broadcast_to(jnp.sum(token_loss, axis=0, keepdims=True), (1, 128))
    for o in range(NY):
        for cx in range(NC):
            if o or cx:
                dev = dp_dev(o, cx)
                rc(lossb.at[me], lossb.at[me], ls_s, ls_r, dev).start()

    def send_terms(o):
        for cx in range(NC):
            for r in range(NX):
                there = (x + r) % NX
                src = xs.at[o, there, pl.ds(cx * TOK, TOK)]
                slot = ((-o) % NY * NC + cx) * NX + (-r) % NX
                if o or cx or r:
                    dev = {"dp": dp_dev(o, cx)["dp"], "vocab": z * NX + there}
                    rc(src, xr.at[slot], x_s, x_r.at[(-o) % NY], dev).start()
                else:
                    xr[0] = xs[0, x, 0:TOK]

    def terms(offsets):
        ga = jnp.concatenate([gv[o].reshape(NC * TOK, VOCAB) for o in offsets], axis=0)
        part = [mm(ga, wv[:, n * 256:(n + 1) * 256], 1, 0) for n in range(2)]
        for n, o in enumerate(offsets):
            rows = slice(n * NC * TOK, (n + 1) * NC * TOK)
            for m in range(NX):
                cols = slice(m * 64, (m + 1) * 64)
                piece = jnp.concatenate([part[0][rows, cols], part[1][rows, cols]], axis=1)
                xs[o, m] = piece.astype(BF16)
            send_terms(o)

    def to_z(o):
        low = o * NC * NX
        came(xr.at[pl.ds(low, 8)] if o else xr.at[pl.ds(1, 7)], x_r.at[o])
        for cx in range(NC):
            val = xr[low + cx * NX].astype(F32)
            for r in range(1, NX):
                val = val + xr[low + cx * NX + r].astype(F32)
            gap = jnp.zeros((8, 128), F32)
            for h in range(2):
                cols = slice(h * 64, (h + 1) * 64)
                part = jnp.concatenate([val[0:24, cols], val[24:48, cols]], axis=1)
                zs[o, cx, h] = jnp.concatenate([part, gap], axis=0).astype(BF16)
                zd = 2 * dp_dev(o, cx)["dp"] + h
                r = (z - zd + NZ) % NZ
                here = r == 0

                @pl.when(jnp.logical_not(here))
                def _():
                    rc(zs.at[o, cx, h], zr.at[r], z_s, z_r, z_dev(zd)).start()

                @pl.when(here)
                def _():
                    zr[0] = zs[o, cx, h]

    def second_halves():
        pass_on(0, 1, 1, 0, 2, 3)
        pass_on(0, 0, 3, 0, 2, 3)

    def far_halves():
        for h in range(2):
            came(gv.at[2, 0, :, half[h]], ag_r.at[4 + h])
            pass_on(2, h, 0, 1, 5, 7)


    @pl.when(c == 0)
    def _():
        gone(gv.at[0, 0], ag_s.at[0])
        second_halves()

    came(gv.at[3, 0, :, half[0]], ag_r.at[0])
    pass_on(3, 0, 1, 0, 3, 4)
    pass_on(3, 0, 0, 1, 4, 6)
    came(gv.at[1, 0, :, half[1]], ag_r.at[1])
    pass_on(1, 1, 3, 0, 3, 5)
    pass_on(1, 1, 0, 1, 4, 6)

    @pl.when(c == 1)
    def _():
        gone(gv.at[0, 0], ag_s.at[0])
        second_halves()

    came(gv.at[0, 1], ag_r.at[2])
    terms((0,))
    came(gv.at[0, 0], ag_r.at[3])
    pass_on(3, 1, 0, 1, 4, 6)
    pass_on(1, 0, 0, 1, 4, 6)
    pl.when(c == 1)(far_halves)
    came(gv.at[0], ag_r.at[6])
    terms((1, 3))
    pl.when(c == 0)(far_halves)
    to_z(0)
    came(gv.at[2, 1], ag_r.at[7])
    terms((2,))

    HB = 256

    def head_copy(n):
        rows = pl.ds(pl.multiple_of(n * HB, HB), HB)
        return pltpu.make_async_copy(head.at[rows], out_head.at[rows], head_sem)

    def head_part(low, high):
        @pl.loop(low, high)
        def _(n):
            rows = pl.ds(pl.multiple_of(n * HB, HB), HB)
            ga = gv[:, :, :, rows].reshape(8 * TOK, HB)
            hb = hv[...].reshape(8 * TOK, FEAT)
            head[rows, :] = mm(ga, hb, 0, 0).astype(BF16)
            head_copy(n).start()

    nh = VOCAB // HB
    head_part(0, 3)
    to_z(3)
    to_z(1)
    head_part(3, 5)
    to_z(2)
    head_part(5, nh)
    came(lossb.at[pl.ds(0, 7)], ls_r)
    loss = lossb[0]
    for k in range(1, 8):
        loss = loss + lossb[k]
    loss_v[...] = loss * (1.0 / (8 * TOK))
    loss_copy = pltpu.make_async_copy(loss_v, out_loss, out_sem.at[0])
    loss_copy.start()


    acc = zr[0].astype(F32)
    came(zr.at[pl.ds(1, NZ - 1)], z_r)
    for r in range(1, NZ):
        acc = acc + zr[r].astype(F32)
    hidden_v[...] = jnp.concatenate([acc[0:24, :64], acc[0:24, 64:]], axis=0).astype(BF16)
    hidden_out = pltpu.make_async_copy(hidden_v, out_hidden, out_sem.at[1])
    hidden_out.start()

    gone(hv.at[0, 1], hs_sem.at[0])
    gone(hv.at[pl.ds(0, 2)], hs_sem.at[1])
    gone(psib, ss_sem)
    gone(enc_opp, rs_s.at[0])
    gone(enc_nb, rs_s.at[1])
    gone(psz.at[pl.ds(0, NZ * NX - 1)], pz_s)
    gone(lossb.at[pl.ds(0, 7)], ls_s)
    gone(gv.at[0, 0], ag_s.at[1])
    gone(gv.at[0, 0], ag_s.at[2])
    gone(gv.at[0, 0], ag_s.at[3])
    gone(gv.at[0], ag_s.at[4])
    gone(gv.at[0, 0], ag_s.at[5])
    gone(xr.at[pl.ds(1, 31)], x_s)
    gone(zr.at[pl.ds(1, NZ - 1)], z_s)
    pltpu.make_async_copy(head, out_head, head_sem).wait()
    loss_copy.wait()
    hidden_out.wait()


def per_device(hidden, head_weight, teacher_ids, teacher_logits):
    vm = pltpu.VMEM
    dma = pltpu.SemaphoreType.DMA
    scratch = [
        vm((TOK, K), jnp.int32),
        vm((TOK, K), F32),
        vm((VOCAB, FEAT), BF16),
        vm((NY, NC, TOK, FEAT), BF16),
        vm((NQ, NY, TOK, QC), F32),
        vm((NQ, NY, TOK, QC), F32),
        vm((NQ, NY, TOK, QC), F32),
        vm((NQ, TOK, QC), jnp.int16),
        vm((NQ, 2, TOK, QC), jnp.int16),
        vm((NQ, TOK, QC), jnp.int16),
        vm((NQ, 2, TOK, QC), jnp.int16),
        vm((TOK, K), F32),
        vm((TOK, NHI, 128), F32),
        vm((NHI, TOK, 128), F32),
        vm((NHI, TOK, 128), F32),
        vm((NZ * NX, 1, 128), F32),
        vm((8, 1, 128), F32),
        vm((NY, NC, TOK, VOCAB), BF16),
        vm((NY, NX, 2 * TOK, 128), BF16),
        vm((NY * NC * NX, TOK, 128), BF16),
        vm((NY, NC, 2, 32, 128), BF16),
        vm((NZ, 32, 128), BF16),
        vm((VOCAB, FEAT), BF16),
        vm((TOK, D // 64), BF16),
        vm((1, 128), F32),
        dma((2,)), dma, dma, dma((3,)), dma((3,)), dma, dma((1 + 2 * NQ,)), dma((2,)), dma((NQ,)), dma((NQ,)),
        dma, dma, dma, dma, dma((6,)), dma((8,)), dma, dma((NY,)), dma, dma, dma, dma((2,)),
        pltpu.SemaphoreType.REGULAR, pltpu.SemaphoreType.REGULAR, pltpu.SemaphoreType.REGULAR,
    ]
    hbm = pl.BlockSpec(memory_space=pltpu.HBM)
    anys = pl.BlockSpec(memory_space=pl.ANY)
    hidden_grad, head_grad, loss = pl.pallas_call(
        kernel,
        out_shape=(
            pltpu.VMEM((TOK, D // 64), BF16),
            pltpu.VMEM((VOCAB, FEAT), BF16),
            pltpu.VMEM((1, 128), F32),
        ),
        in_specs=[hbm, hbm, hbm, hbm],
        out_specs=(anys, anys, anys),
        scratch_shapes=scratch,
        compiler_params=pltpu.CompilerParams(
            collective_id=0, has_side_effects=True, vmem_limit_bytes=56 * 1024 * 1024
        ),
    )(hidden, head_weight, teacher_ids, teacher_logits)
    return hidden_grad, head_grad, loss[0, 0]


def solution(mesh):
    in_specs = (P("dp", None), P("vocab", "dp"), P("dp", None), P("dp", None))
    out_specs = (P("dp", "vocab"), P("vocab", "dp"), P())
    return jax.shard_map(
        per_device, mesh=mesh, in_specs=in_specs, out_specs=out_specs, check_vma=False
    )
```

```python
import jax
import jax.numpy as jnp
from jax import lax
from jax.experimental import pallas as pl
from jax.experimental.pallas import tpu as pltpu
from jax.sharding import PartitionSpec as P

MESH = pl.DeviceIdType.MESH
F32 = jnp.float32
BF16 = jnp.bfloat16
soft_cap = 30.0

NY, NC, NX, NZ = 4, 2, 4, 16
TOK, D, K = 48, 4096, 256
FEAT = D // 8
VOCAB = 131072 // 64
NQ = 4
QC = VOCAB // NQ
NHI = VOCAB // 128
BEND = 48.0
LEVELS = 32767.0


def encode(x):
    return jnp.round(x * (LEVELS / (jnp.abs(x) + BEND))).astype(jnp.int32).astype(jnp.int16)


def decode(q):
    u = q.astype(jnp.int32).astype(F32)
    return u * (BEND / (LEVELS - jnp.abs(u)))


def mm(a, b, ca, cb):
    return lax.dot_general(a, b, (((ca,), (cb,)), ((), ())), preferred_element_type=F32)


def kernel(
    hidden, weight, ids_in, logits_in, out_hidden, out_head, out_loss,
    ids, logits, wv, hv, psib, pown, srecv, enc_opp, enc_nb, in_opp, in_nb,
    prob, tgt, es, om, psz, lossb, gv, xs, xr, zs, zr, head, hidden_v, loss_v,
    id_sem, w_sem, own_sem, hs_sem, hr_sem, ss_sem, sr_sem, rs_s, rs_opp, rs_nb,
    pz_s, pz_r, ls_s, ls_r, ag_s, ag_r, x_s, x_r, z_s, z_r, head_sem, out_sem, near2, near4, near8,
):
    me = lax.axis_index("dp")
    vo = lax.axis_index("vocab")
    y, c = me // 2, me % 2
    z, x = vo // NX, vo % NX

    def dp_dev(o, cx):
        return {"dp": ((y + o) % NY) * 2 + (c + cx) % 2, "vocab": vo}

    def x_dev(r):
        return {"dp": me, "vocab": z * NX + (x + r) % NX}

    def z_dev(zz):
        return {"dp": me, "vocab": zz * NX + x}

    def rc(src, dst, ssem, rsem, dev):
        return pltpu.make_async_remote_copy(
            src_ref=src, dst_ref=dst, send_sem=ssem, recv_sem=rsem, device_id=dev, device_id_type=MESH
        )


    def came(ref, sem):
        rc(ref, ref, hs_sem.at[0], sem, dp_dev(0, 1)).wait_recv()

    def gone(ref, sem):
        rc(ref, ref, sem, hr_sem.at[0], dp_dev(0, 1)).wait_send()

    barrier = pltpu.get_barrier_semaphore()

    def greet(dev):
        pl.semaphore_signal(barrier, inc=1, device_id=dev, device_id_type=MESH)

    for o in range(NY):
        for cx in range(NC):
            if o or cx:
                greet(dp_dev(o, cx))
    for r in range(1, NX):
        greet(x_dev(r))
    for r in (1, 2, NZ - 2, NZ - 1):
        greet(z_dev((z + r) % NZ))

    w_copy = pltpu.make_async_copy(weight, wv, w_sem)
    own_h = pltpu.make_async_copy(hidden.at[:, pl.ds(pl.multiple_of(me * FEAT, FEAT), FEAT)], hv.at[0, 0], own_sem)
    own_h.start()
    id_copies = [
        pltpu.make_async_copy(ids_in, ids, id_sem.at[0]), pltpu.make_async_copy(logits_in, logits, id_sem.at[1])
    ]
    for w in id_copies:
        w.start()
    w_copy.start()

    pl.semaphore_wait(barrier, 7 + (NX - 1) + 4)

    def tell(sem, *steps):
        for step in steps:
            for r in (step, NZ - step):
                pl.semaphore_signal(sem, inc=1, device_id=z_dev((z + r) % NZ), device_id_type=MESH)


    def hidden_copy(o, cx):
        dev = dp_dev(o, cx)
        back = (-o) % NY
        cols = pl.ds(pl.multiple_of(dev["dp"] * FEAT, FEAT), FEAT)
        n = (0, 1, 2, 1)[o]
        return rc(hidden.at[:, cols], hv.at[back, cx], hs_sem.at[n], hr_sem.at[n], dev)

    for o, cx in ((2, 0), (2, 1), (0, 1)):
        hidden_copy(o, cx).start()
    tell(near2, 1, 2)
    for r in range(1, NX):
        pl.semaphore_signal(near2, inc=1, device_id=x_dev(r), device_id_type=MESH)

    for w in id_copies:
        w.wait()
    lg = logits[...]
    logp = lg - jnp.log(jnp.sum(jnp.exp(lg), axis=1, keepdims=True))
    pr = jnp.exp(logp)
    prob[...] = pr
    entropy = jnp.sum(pr * logp, axis=1, keepdims=True)

    first = vo * VOCAB
    rows16 = lax.broadcasted_iota(jnp.int32, (NHI, K), 0)
    rows128 = lax.broadcasted_iota(jnp.int32, (128, K), 0)

    def target_tokens(n):
        for k in range(4):
            t = n * 4 + k
            place = ids[pl.ds(t, 1), :] - first
            p = prob[pl.ds(t, 1), :]
            a = jnp.where((place >> 7) == rows16, p, 0.0)
            a1 = a.astype(BF16)
            rest = a - a1.astype(F32)
            a2 = rest.astype(BF16)
            a3 = (rest - a2.astype(F32)).astype(BF16)
            b = jnp.where((place & 127) == rows128, 1.0, 0.0).astype(BF16)
            both = mm(jnp.concatenate([a1, a2, a3], axis=0), b, 1, 1)
            tgt[t] = both[0:NHI] + both[NHI:2 * NHI] + both[2 * NHI:3 * NHI]

    pl.loop(0, 8)(target_tokens)
    for o, cx in ((1, 0), (3, 0), (1, 1), (3, 1)):
        hidden_copy(o, cx).start()

    place_of = (0, 2, 1, 3)

    def partial_logits(q, offsets):
        hb = jnp.concatenate([hv[o].reshape(NC * TOK, FEAT) for o in offsets], axis=0)
        part = mm(hb, wv[pl.ds(pl.multiple_of(q * QC, QC), QC), :], 1, 1)
        for n, o in enumerate(offsets):
            pown[q, place_of[o]] = part[2 * n * TOK:(2 * n + 1) * TOK]
            psib[q, place_of[o]] = part[(2 * n + 1) * TOK:(2 * n + 2) * TOK]

    def sib_copy(q, offsets):
        places = pl.ds(place_of[offsets[0]], len(offsets))
        n = 0 if offsets == (0,) else 1 + q + NQ * (len(offsets) - 1)
        return rc(psib.at[q, places], srecv.at[q, places], ss_sem, sr_sem.at[n], dp_dev(0, 1))

    def q_of(s):
        return (s % 2) * 2 + s // 2

    def way(q):
        return 1 + 2 * (q // 2)

    def opp_copy(q):
        return rc(enc_opp.at[q], in_opp.at[q], rs_s.at[0], rs_opp.at[q], dp_dev(way(q), 0))

    def nb_copy(q, o):
        slot, back = o // 2, 1 - o // 2
        return rc(enc_nb.at[q, slot], in_nb.at[q, back], rs_s.at[1], rs_nb.at[q], dp_dev(o, 0))

    w_copy.wait()
    own_h.wait()
    came(hv.at[0, 1], hr_sem.at[0])

    @pl.loop(0, NQ)
    def _(q):
        partial_logits(q, (0,))
        sib_copy(q, (0,)).start()

    pl.loop(8, TOK // 4)(target_tokens)
    pl.semaphore_wait(near2, 4 + NX - 1)
    tell(near4, 4)
    came(hv.at[2], hr_sem.at[2])

    @pl.loop(0, NQ)
    def _(s):
        q = q_of(s)
        partial_logits(q, (2,))
        sib_copy(q, (2,)).start()


    @pl.loop(0, NQ)
    def _(s):
        q = q_of(s)
        sib_copy(q, (2,)).wait_recv()
        enc_opp[q] = encode(pown[q, 1] + srecv[q, 1])
        opp_copy(q).start()

    came(hv.at[pl.ds(0, 2)], hr_sem.at[1])

    @pl.loop(0, NQ + 3)
    def _(s):
        @pl.when(s < NQ)
        def _():
            q = q_of(s)
            partial_logits(q, (1, 3))
            sib_copy(q, (1, 3)).start()

        @pl.when(jnp.logical_and(s > 1, s <= NQ + 1))
        def _():
            q = q_of(s - 2)
            sib_copy(q, (1, 3)).wait_recv()
            o = 4 - way(q)
            enc_nb[q, o // 2] = encode(pown[q, 2 + o // 2] + srecv[q, 2 + o // 2])
            nb_copy(q, o).start()

        @pl.when(s > 2)
        def _():
            q = q_of(s - 3)
            opp_copy(q).wait_recv()
            o = way(q)
            enc_nb[q, o // 2] = encode(pown[q, 2 + o // 2] + srecv[q, 2 + o // 2] + decode(in_opp[q]))
            nb_copy(q, o).start()

    pl.semaphore_wait(near4, 2)
    tell(near8, 4)
    tot = jnp.zeros((TOK, 128), F32)
    crs = jnp.zeros((TOK, 128), F32)
    came(srecv.at[:, 0], sr_sem.at[0])
    for s in range(NQ):
        q = q_of(s)
        came(in_nb.at[q], rs_nb.at[q])
        for k in range(QC // 128):
            cols = slice(k * 128, (k + 1) * 128)
            hi = q * (QC // 128) + k
            raw = (
                pown[q, 0, :, cols] + srecv[q, 0, :, cols]
                + decode(in_nb[q, 0, :, cols]) + decode(in_nb[q, 1, :, cols])
            )
            squash = jnp.tanh(raw * (1.0 / soft_cap))
            student = soft_cap * squash
            expo = jnp.exp(student)
            es[hi] = expo
            om[hi] = 1.0 - squash * squash
            tot = tot + expo
            crs = crs + tgt[:, hi, :] * student

    lane = lax.broadcasted_iota(jnp.int32, (TOK, 128), 1)
    row = lax.broadcasted_iota(jnp.int32, (TOK, 128), 0)
    mine = jnp.where(lane == row, jnp.sum(tot, axis=1, keepdims=True), 0.0) + jnp.where(
        lane == row + 64, jnp.sum(crs, axis=1, keepdims=True), 0.0
    )
    psz[vo] = jnp.sum(mine, axis=0, keepdims=True)
    pl.semaphore_wait(near8, 2)

    @pl.loop(0, NZ * NX - 1)
    def _(n):
        there = (vo + NZ * NX // 2 + (1 - 2 * (n % 2)) * ((n + 1) // 2)) % (NZ * NX)
        rc(psz.at[vo], psz.at[vo], pz_s, pz_r, {"dp": me, "vocab": there}).start()

    came(psz.at[pl.ds(0, NZ * NX - 1)], pz_r)
    sums = jnp.sum(psz[...], axis=0)
    sums = jnp.broadcast_to(sums, (TOK, 128))
    total = jnp.sum(jnp.where(lane == row, sums, 0.0), axis=1, keepdims=True)
    cross = jnp.sum(jnp.where(lane == row + 64, sums, 0.0), axis=1, keepdims=True)
    inv = 1.0 / total
    for hi in range(NHI):
        g = (es[hi] * inv - tgt[:, hi, :]) * om[hi]
        gv[0, 0, :, hi * 128:(hi + 1) * 128] = g.astype(BF16)

    half = [pl.ds(0, VOCAB // 2), pl.ds(VOCAB // 2, VOCAB // 2)]

    def pass_on(o, h, do, dcx, ssem, rsem):
        back = (o - do) % NY
        src = gv.at[o, 0] if h is None else gv.at[o, 0, :, half[h]]
        dst = gv.at[back, dcx] if h is None else gv.at[back, dcx, :, half[h]]
        rc(src, dst, ag_s.at[ssem], ag_r.at[rsem], dp_dev(do, dcx)).start()

    pass_on(0, 0, 1, 0, 0, 0)
    pass_on(0, 1, 3, 0, 0, 1)
    pass_on(0, None, 0, 1, 1, 2)

    token_loss = entropy - cross + jnp.log(total)
    lossb[me] = jnp.broadcast_to(jnp.sum(token_loss, axis=0, keepdims=True), (1, 128))
    for o in range(NY):
        for cx in range(NC):
            if o or cx:
                dev = dp_dev(o, cx)
                rc(lossb.at[me], lossb.at[me], ls_s, ls_r, dev).start()

    def send_terms(o):
        for cx in range(NC):
            for r in range(NX):
                there = (x + r) % NX
                src = xs.at[o, there, pl.ds(cx * TOK, TOK)]
                slot = ((-o) % NY * NC + cx) * NX + (-r) % NX
                if o or cx or r:
                    dev = {"dp": dp_dev(o, cx)["dp"], "vocab": z * NX + there}
                    rc(src, xr.at[slot], x_s, x_r.at[(-o) % NY], dev).start()
                else:
                    xr[0] = xs[0, x, 0:TOK]

    def terms(offsets):
        ga = jnp.concatenate([gv[o].reshape(NC * TOK, VOCAB) for o in offsets], axis=0)
        part = [mm(ga, wv[:, n * 256:(n + 1) * 256], 1, 0) for n in range(2)]
        for n, o in enumerate(offsets):
            rows = slice(n * NC * TOK, (n + 1) * NC * TOK)
            for m in range(NX):
                cols = slice(m * 64, (m + 1) * 64)
                piece = jnp.concatenate([part[0][rows, cols], part[1][rows, cols]], axis=1)
                xs[o, m] = piece.astype(BF16)
            send_terms(o)

    def to_z(o):
        low = o * NC * NX
        came(xr.at[pl.ds(low, 8)] if o else xr.at[pl.ds(1, 7)], x_r.at[o])
        for cx in range(NC):
            val = xr[low + cx * NX].astype(F32)
            for r in range(1, NX):
                val = val + xr[low + cx * NX + r].astype(F32)
            gap = jnp.zeros((8, 128), F32)
            for h in range(2):
                cols = slice(h * 64, (h + 1) * 64)
                part = jnp.concatenate([val[0:24, cols], val[24:48, cols]], axis=1)
                zs[o, cx, h] = jnp.concatenate([part, gap], axis=0).astype(BF16)
                zd = 2 * dp_dev(o, cx)["dp"] + h
                r = (z - zd + NZ) % NZ
                here = r == 0

                @pl.when(jnp.logical_not(here))
                def _():
                    rc(zs.at[o, cx, h], zr.at[r], z_s, z_r, z_dev(zd)).start()

                @pl.when(here)
                def _():
                    zr[0] = zs[o, cx, h]

    def second_halves():
        pass_on(0, 1, 1, 0, 2, 3)
        pass_on(0, 0, 3, 0, 2, 3)

    def far_halves():
        for h in range(2):
            came(gv.at[2, 0, :, half[h]], ag_r.at[4 + h])
            pass_on(2, h, 0, 1, 5, 7)


    def terms_own():
        came(gv.at[0, 1], ag_r.at[2])
        terms((0,))

    pl.when(c == 1)(second_halves)

    @pl.when(c == 0)
    def _():
        terms_own()
        second_halves()

    came(gv.at[3, 0, :, half[0]], ag_r.at[0])
    pass_on(3, 0, 1, 0, 3, 4)
    pass_on(3, 0, 0, 1, 4, 6)
    came(gv.at[1, 0, :, half[1]], ag_r.at[1])
    pass_on(1, 1, 3, 0, 3, 5)
    pass_on(1, 1, 0, 1, 4, 6)
    pl.when(c == 1)(terms_own)
    came(gv.at[0, 0], ag_r.at[3])
    pass_on(3, 1, 0, 1, 4, 6)
    pass_on(1, 0, 0, 1, 4, 6)
    pl.when(c == 1)(far_halves)
    came(gv.at[0], ag_r.at[6])
    terms((1, 3))
    pl.when(c == 0)(far_halves)
    to_z(0)
    came(gv.at[2, 1], ag_r.at[7])
    terms((2,))

    HB = 256

    def head_copy(n):
        rows = pl.ds(pl.multiple_of(n * HB, HB), HB)
        return pltpu.make_async_copy(head.at[rows], out_head.at[rows], head_sem)

    def head_part(low, high):
        @pl.loop(low, high)
        def _(n):
            rows = pl.ds(pl.multiple_of(n * HB, HB), HB)
            ga = gv[:, :, :, rows].reshape(8 * TOK, HB)
            hb = hv[...].reshape(8 * TOK, FEAT)
            head[rows, :] = mm(ga, hb, 0, 0).astype(BF16)
            head_copy(n).start()

    nh = VOCAB // HB
    head_part(0, 3)
    to_z(3)
    to_z(1)
    head_part(3, 5)
    to_z(2)
    head_part(5, nh)
    came(lossb.at[pl.ds(0, 7)], ls_r)
    loss = lossb[0]
    for k in range(1, 8):
        loss = loss + lossb[k]
    loss_v[...] = loss * (1.0 / (8 * TOK))
    loss_copy = pltpu.make_async_copy(loss_v, out_loss, out_sem.at[0])
    loss_copy.start()


    acc = zr[0].astype(F32)
    came(zr.at[pl.ds(1, NZ - 1)], z_r)
    for r in range(1, NZ):
        acc = acc + zr[r].astype(F32)
    hidden_v[...] = jnp.concatenate([acc[0:24, :64], acc[0:24, 64:]], axis=0).astype(BF16)
    hidden_out = pltpu.make_async_copy(hidden_v, out_hidden, out_sem.at[1])
    hidden_out.start()

    gone(hv.at[0, 1], hs_sem.at[0])
    gone(hv.at[0], hs_sem.at[2])
    gone(hv.at[pl.ds(0, 2)], hs_sem.at[1])
    gone(psib, ss_sem)
    gone(enc_opp, rs_s.at[0])
    gone(enc_nb, rs_s.at[1])
    gone(psz.at[pl.ds(0, NZ * NX - 1)], pz_s)
    gone(lossb.at[pl.ds(0, 7)], ls_s)
    gone(gv.at[0, 0], ag_s.at[0])
    gone(gv.at[0, 0], ag_s.at[1])
    gone(gv.at[0, 0], ag_s.at[2])
    gone(gv.at[0, 0], ag_s.at[3])
    gone(gv.at[0], ag_s.at[4])
    gone(gv.at[0, 0], ag_s.at[5])
    gone(xr.at[pl.ds(1, 31)], x_s)
    gone(zr.at[pl.ds(1, NZ - 1)], z_s)
    pltpu.make_async_copy(head, out_head, head_sem).wait()
    loss_copy.wait()
    hidden_out.wait()


def per_device(hidden, head_weight, teacher_ids, teacher_logits):
    vm = pltpu.VMEM
    dma = pltpu.SemaphoreType.DMA
    scratch = [
        vm((TOK, K), jnp.int32),
        vm((TOK, K), F32),
        vm((VOCAB, FEAT), BF16),
        vm((NY, NC, TOK, FEAT), BF16),
        vm((NQ, NY, TOK, QC), F32),
        vm((NQ, NY, TOK, QC), F32),
        vm((NQ, NY, TOK, QC), F32),
        vm((NQ, TOK, QC), jnp.int16),
        vm((NQ, 2, TOK, QC), jnp.int16),
        vm((NQ, TOK, QC), jnp.int16),
        vm((NQ, 2, TOK, QC), jnp.int16),
        vm((TOK, K), F32),
        vm((TOK, NHI, 128), F32),
        vm((NHI, TOK, 128), F32),
        vm((NHI, TOK, 128), F32),
        vm((NZ * NX, 1, 128), F32),
        vm((8, 1, 128), F32),
        vm((NY, NC, TOK, VOCAB), BF16),
        vm((NY, NX, 2 * TOK, 128), BF16),
        vm((NY * NC * NX, TOK, 128), BF16),
        vm((NY, NC, 2, 32, 128), BF16),
        vm((NZ, 32, 128), BF16),
        vm((VOCAB, FEAT), BF16),
        vm((TOK, D // 64), BF16),
        vm((1, 128), F32),
        dma((2,)), dma, dma, dma((3,)), dma((3,)), dma, dma((1 + 2 * NQ,)), dma((2,)), dma((NQ,)), dma((NQ,)),
        dma, dma, dma, dma, dma((6,)), dma((8,)), dma, dma((NY,)), dma, dma, dma, dma((2,)),
        pltpu.SemaphoreType.REGULAR, pltpu.SemaphoreType.REGULAR, pltpu.SemaphoreType.REGULAR,
    ]
    hbm = pl.BlockSpec(memory_space=pltpu.HBM)
    anys = pl.BlockSpec(memory_space=pl.ANY)
    hidden_grad, head_grad, loss = pl.pallas_call(
        kernel,
        out_shape=(
            pltpu.VMEM((TOK, D // 64), BF16),
            pltpu.VMEM((VOCAB, FEAT), BF16),
            pltpu.VMEM((1, 128), F32),
        ),
        in_specs=[hbm, hbm, hbm, hbm],
        out_specs=(anys, anys, anys),
        scratch_shapes=scratch,
        compiler_params=pltpu.CompilerParams(
            collective_id=0, has_side_effects=True, vmem_limit_bytes=56 * 1024 * 1024
        ),
    )(hidden, head_weight, teacher_ids, teacher_logits)
    return hidden_grad, head_grad, loss[0, 0]


def solution(mesh):
    in_specs = (P("dp", None), P("vocab", "dp"), P("dp", None), P("dp", None))
    out_specs = (P("dp", "vocab"), P("vocab", "dp"), P())
    return jax.shard_map(
        per_device, mesh=mesh, in_specs=in_specs, out_specs=out_specs, check_vma=False
    )
```

```python
import jax
import jax.numpy as jnp
from jax import lax
from jax.experimental import pallas as pl
from jax.experimental.pallas import tpu as pltpu
from jax.sharding import PartitionSpec as P

MESH = pl.DeviceIdType.MESH
F32 = jnp.float32
BF16 = jnp.bfloat16
soft_cap = 30.0

NY, NC, NX, NZ = 4, 2, 4, 16
TOK, D, K = 48, 4096, 256
FEAT = D // 8
VOCAB = 131072 // 64
NQ = 4
QC = VOCAB // NQ
NHI = VOCAB // 128
BEND = 48.0
LEVELS = 32767.0


def encode(x):
    return jnp.round(x * (LEVELS / (jnp.abs(x) + BEND))).astype(jnp.int32).astype(jnp.int16)


def decode(q):
    u = q.astype(jnp.int32).astype(F32)
    return u * (BEND / (LEVELS - jnp.abs(u)))


def mm(a, b, ca, cb):
    return lax.dot_general(a, b, (((ca,), (cb,)), ((), ())), preferred_element_type=F32)


def kernel(
    hidden, weight, ids_in, logits_in, out_small, out_head,
    ids, logits, wv, hv, psib, pown, srecv, enc_opp, enc_nb, in_opp, in_nb,
    prob, tgt, es, om, psz, lossb, gv, xs, xr, zs, zr, head,
    id_sem, w_sem, own_sem, hs_sem, hr_sem, ss_sem, sr_sem, rs_s, rs_opp, rs_nb,
    pz_s, pz_r, ls_s, ls_r, ag_s, ag_r, x_s, x_r, z_s, z_r, head_sem, near2, near4, near8,
):
    me = lax.axis_index("dp")
    vo = lax.axis_index("vocab")
    y, c = me // 2, me % 2
    z, x = vo // NX, vo % NX

    def dp_dev(o, cx):
        return {"dp": ((y + o) % NY) * 2 + (c + cx) % 2, "vocab": vo}

    def x_dev(r):
        return {"dp": me, "vocab": z * NX + (x + r) % NX}

    def z_dev(zz):
        return {"dp": me, "vocab": zz * NX + x}

    def rc(src, dst, ssem, rsem, dev):
        return pltpu.make_async_remote_copy(
            src_ref=src, dst_ref=dst, send_sem=ssem, recv_sem=rsem, device_id=dev, device_id_type=MESH
        )


    def came(ref, sem):
        rc(ref, ref, hs_sem.at[0], sem, dp_dev(0, 1)).wait_recv()

    def gone(ref, sem):
        rc(ref, ref, sem, hr_sem.at[0], dp_dev(0, 1)).wait_send()

    barrier = pltpu.get_barrier_semaphore()

    def greet(dev):
        pl.semaphore_signal(barrier, inc=1, device_id=dev, device_id_type=MESH)

    for o in range(NY):
        for cx in range(NC):
            if o or cx:
                greet(dp_dev(o, cx))
    for r in range(1, NX):
        greet(x_dev(r))
    for r in (1, 2, NZ - 2, NZ - 1):
        greet(z_dev((z + r) % NZ))

    w_copy = pltpu.make_async_copy(weight, wv, w_sem)
    own_h = pltpu.make_async_copy(hidden.at[:, pl.ds(pl.multiple_of(me * FEAT, FEAT), FEAT)], hv.at[0, 0], own_sem)
    own_h.start()
    id_copies = [
        pltpu.make_async_copy(ids_in, ids, id_sem.at[0]), pltpu.make_async_copy(logits_in, logits, id_sem.at[1])
    ]
    for w in id_copies:
        w.start()
    w_copy.start()

    pl.semaphore_wait(barrier, 7 + (NX - 1) + 4)

    def tell(sem, *steps):
        for step in steps:
            for r in (step, NZ - step):
                pl.semaphore_signal(sem, inc=1, device_id=z_dev((z + r) % NZ), device_id_type=MESH)


    def hidden_copy(o, cx):
        dev = dp_dev(o, cx)
        back = (-o) % NY
        cols = pl.ds(pl.multiple_of(dev["dp"] * FEAT, FEAT), FEAT)
        n = (0, 1, 2, 1)[o]
        return rc(hidden.at[:, cols], hv.at[back, cx], hs_sem.at[n], hr_sem.at[n], dev)

    for o, cx in ((2, 0), (2, 1), (0, 1)):
        hidden_copy(o, cx).start()
    tell(near2, 1, 2)
    for r in range(1, NX):
        pl.semaphore_signal(near2, inc=1, device_id=x_dev(r), device_id_type=MESH)

    for w in id_copies:
        w.wait()
    lg = logits[...]
    logp = lg - jnp.log(jnp.sum(jnp.exp(lg), axis=1, keepdims=True))
    pr = jnp.exp(logp)
    prob[...] = pr
    entropy = jnp.sum(pr * logp, axis=1, keepdims=True)

    first = vo * VOCAB
    rows16 = lax.broadcasted_iota(jnp.int32, (NHI, K), 0)
    rows128 = lax.broadcasted_iota(jnp.int32, (128, K), 0)

    def target_tokens(n):
        for k in range(4):
            t = n * 4 + k
            place = ids[pl.ds(t, 1), :] - first
            p = prob[pl.ds(t, 1), :]
            a = jnp.where((place >> 7) == rows16, p, 0.0)
            a1 = a.astype(BF16)
            rest = a - a1.astype(F32)
            a2 = rest.astype(BF16)
            a3 = (rest - a2.astype(F32)).astype(BF16)
            b = jnp.where((place & 127) == rows128, 1.0, 0.0).astype(BF16)
            both = mm(jnp.concatenate([a1, a2, a3], axis=0), b, 1, 1)
            tgt[t] = both[0:NHI] + both[NHI:2 * NHI] + both[2 * NHI:3 * NHI]

    pl.loop(0, 8)(target_tokens)
    for o, cx in ((1, 0), (3, 0), (1, 1), (3, 1)):
        hidden_copy(o, cx).start()

    place_of = (0, 2, 1, 3)

    def partial_logits(q, offsets):
        hb = jnp.concatenate([hv[o].reshape(NC * TOK, FEAT) for o in offsets], axis=0)
        part = mm(hb, wv[pl.ds(pl.multiple_of(q * QC, QC), QC), :], 1, 1)
        for n, o in enumerate(offsets):
            pown[q, place_of[o]] = part[2 * n * TOK:(2 * n + 1) * TOK]
            psib[q, place_of[o]] = part[(2 * n + 1) * TOK:(2 * n + 2) * TOK]

    def sib_copy(q, offsets):
        places = pl.ds(place_of[offsets[0]], len(offsets))
        n = 0 if offsets == (0,) else 1 + q + NQ * (len(offsets) - 1)
        return rc(psib.at[q, places], srecv.at[q, places], ss_sem, sr_sem.at[n], dp_dev(0, 1))

    def q_of(s):
        return (s % 2) * 2 + s // 2

    def way(q):
        return 1 + 2 * (q // 2)

    def opp_copy(q):
        return rc(enc_opp.at[q], in_opp.at[q], rs_s.at[0], rs_opp.at[q], dp_dev(way(q), 0))

    def nb_copy(q, o):
        slot, back = o // 2, 1 - o // 2
        return rc(enc_nb.at[q, slot], in_nb.at[q, back], rs_s.at[1], rs_nb.at[q], dp_dev(o, 0))

    w_copy.wait()
    own_h.wait()
    came(hv.at[0, 1], hr_sem.at[0])

    @pl.loop(0, NQ)
    def _(q):
        partial_logits(q, (0,))
        sib_copy(q, (0,)).start()

    pl.loop(8, TOK // 4)(target_tokens)
    pl.semaphore_wait(near2, 4 + NX - 1)
    tell(near4, 4)
    came(hv.at[2], hr_sem.at[2])

    @pl.loop(0, NQ)
    def _(s):
        q = q_of(s)
        partial_logits(q, (2,))
        sib_copy(q, (2,)).start()


    @pl.loop(0, NQ)
    def _(s):
        q = q_of(s)
        sib_copy(q, (2,)).wait_recv()
        enc_opp[q] = encode(pown[q, 1] + srecv[q, 1])
        opp_copy(q).start()

    came(hv.at[pl.ds(0, 2)], hr_sem.at[1])

    @pl.loop(0, NQ + 3)
    def _(s):
        @pl.when(s < NQ)
        def _():
            q = q_of(s)
            partial_logits(q, (1, 3))
            sib_copy(q, (1, 3)).start()

        @pl.when(jnp.logical_and(s > 1, s <= NQ + 1))
        def _():
            q = q_of(s - 2)
            sib_copy(q, (1, 3)).wait_recv()
            o = 4 - way(q)
            enc_nb[q, o // 2] = encode(pown[q, 2 + o // 2] + srecv[q, 2 + o // 2])
            nb_copy(q, o).start()

        @pl.when(s > 2)
        def _():
            q = q_of(s - 3)
            opp_copy(q).wait_recv()
            o = way(q)
            enc_nb[q, o // 2] = encode(pown[q, 2 + o // 2] + srecv[q, 2 + o // 2] + decode(in_opp[q]))
            nb_copy(q, o).start()

    pl.semaphore_wait(near4, 2)
    tell(near8, 4)
    tot = jnp.zeros((TOK, 128), F32)
    crs = jnp.zeros((TOK, 128), F32)
    came(srecv.at[:, 0], sr_sem.at[0])
    for s in range(NQ):
        q = q_of(s)
        came(in_nb.at[q], rs_nb.at[q])
        for k in range(QC // 128):
            cols = slice(k * 128, (k + 1) * 128)
            hi = q * (QC // 128) + k
            raw = (
                pown[q, 0, :, cols] + srecv[q, 0, :, cols]
                + decode(in_nb[q, 0, :, cols]) + decode(in_nb[q, 1, :, cols])
            )
            squash = jnp.tanh(raw * (1.0 / soft_cap))
            student = soft_cap * squash
            expo = jnp.exp(student)
            es[hi] = expo
            om[hi] = 1.0 - squash * squash
            tot = tot + expo
            crs = crs + tgt[:, hi, :] * student

    lane = lax.broadcasted_iota(jnp.int32, (TOK, 128), 1)
    row = lax.broadcasted_iota(jnp.int32, (TOK, 128), 0)
    mine = jnp.where(lane == row, jnp.sum(tot, axis=1, keepdims=True), 0.0) + jnp.where(
        lane == row + 64, jnp.sum(crs, axis=1, keepdims=True), 0.0
    )
    psz[vo] = jnp.sum(mine, axis=0, keepdims=True)
    pl.semaphore_wait(near8, 2)

    @pl.loop(0, NZ * NX - 1)
    def _(n):
        there = (vo + NZ * NX // 2 + (1 - 2 * (n % 2)) * ((n + 1) // 2)) % (NZ * NX)
        rc(psz.at[vo], psz.at[vo], pz_s, pz_r, {"dp": me, "vocab": there}).start()

    came(psz.at[pl.ds(0, NZ * NX - 1)], pz_r)
    sums = jnp.sum(psz[...], axis=0)
    sums = jnp.broadcast_to(sums, (TOK, 128))
    total = jnp.sum(jnp.where(lane == row, sums, 0.0), axis=1, keepdims=True)
    cross = jnp.sum(jnp.where(lane == row + 64, sums, 0.0), axis=1, keepdims=True)
    inv = 1.0 / total
    for hi in range(NHI):
        g = (es[hi] * inv - tgt[:, hi, :]) * om[hi]
        gv[0, 0, :, hi * 128:(hi + 1) * 128] = g.astype(BF16)

    half = [pl.ds(0, VOCAB // 2), pl.ds(VOCAB // 2, VOCAB // 2)]

    def pass_on(o, h, do, dcx, ssem, rsem):
        back = (o - do) % NY
        src = gv.at[o, 0] if h is None else gv.at[o, 0, :, half[h]]
        dst = gv.at[back, dcx] if h is None else gv.at[back, dcx, :, half[h]]
        rc(src, dst, ag_s.at[ssem], ag_r.at[rsem], dp_dev(do, dcx)).start()

    pass_on(0, 0, 1, 0, 0, 0)
    pass_on(0, 1, 3, 0, 0, 1)
    pass_on(0, None, 0, 1, 1, 2)

    token_loss = entropy - cross + jnp.log(total)
    lossb[me] = jnp.broadcast_to(jnp.sum(token_loss, axis=0, keepdims=True), (1, 128))
    for o in range(NY):
        for cx in range(NC):
            if o or cx:
                dev = dp_dev(o, cx)
                rc(lossb.at[me], lossb.at[me], ls_s, ls_r, dev).start()

    def send_terms(o):
        for cx in range(NC):
            for r in range(NX):
                there = (x + r) % NX
                src = xs.at[o, there, pl.ds(cx * TOK, TOK)]
                slot = ((-o) % NY * NC + cx) * NX + (-r) % NX
                if o or cx or r:
                    dev = {"dp": dp_dev(o, cx)["dp"], "vocab": z * NX + there}
                    rc(src, xr.at[slot], x_s, x_r.at[(-o) % NY], dev).start()
                else:
                    xr[0] = xs[0, x, 0:TOK]

    def terms(offsets):
        ga = jnp.concatenate([gv[o].reshape(NC * TOK, VOCAB) for o in offsets], axis=0)
        part = [mm(ga, wv[:, n * 256:(n + 1) * 256], 1, 0) for n in range(2)]
        for n, o in enumerate(offsets):
            rows = slice(n * NC * TOK, (n + 1) * NC * TOK)
            for m in range(NX):
                cols = slice(m * 64, (m + 1) * 64)
                piece = jnp.concatenate([part[0][rows, cols], part[1][rows, cols]], axis=1)
                xs[o, m] = piece.astype(BF16)
            send_terms(o)

    def to_z(o):
        low = o * NC * NX
        came(xr.at[pl.ds(low, 8)] if o else xr.at[pl.ds(1, 7)], x_r.at[o])
        for cx in range(NC):
            val = xr[low + cx * NX].astype(F32)
            for r in range(1, NX):
                val = val + xr[low + cx * NX + r].astype(F32)
            gap = jnp.zeros((8, 128), F32)
            for h in range(2):
                cols = slice(h * 64, (h + 1) * 64)
                part = jnp.concatenate([val[0:24, cols], val[24:48, cols]], axis=1)
                zs[o, cx, h] = jnp.concatenate([part, gap], axis=0).astype(BF16)
                zd = 2 * dp_dev(o, cx)["dp"] + h
                r = (z - zd + NZ) % NZ
                here = r == 0

                @pl.when(jnp.logical_not(here))
                def _():
                    rc(zs.at[o, cx, h], zr.at[r], z_s, z_r, z_dev(zd)).start()

                @pl.when(here)
                def _():
                    zr[0] = zs[o, cx, h]

    def second_halves():
        pass_on(0, 1, 1, 0, 2, 3)
        pass_on(0, 0, 3, 0, 2, 3)

    def far_halves():
        for h in range(2):
            came(gv.at[2, 0, :, half[h]], ag_r.at[4 + h])
            pass_on(2, h, 0, 1, 5, 7)


    def terms_own():
        came(gv.at[0, 1], ag_r.at[2])
        terms((0,))

    pl.when(c == 1)(second_halves)

    @pl.when(c == 0)
    def _():
        terms_own()
        second_halves()

    came(gv.at[3, 0, :, half[0]], ag_r.at[0])
    pass_on(3, 0, 1, 0, 3, 4)
    pass_on(3, 0, 0, 1, 4, 6)
    came(gv.at[1, 0, :, half[1]], ag_r.at[1])
    pass_on(1, 1, 3, 0, 3, 5)
    pass_on(1, 1, 0, 1, 4, 6)
    pl.when(c == 1)(terms_own)
    came(gv.at[0, 0], ag_r.at[3])
    pass_on(3, 1, 0, 1, 4, 6)
    pass_on(1, 0, 0, 1, 4, 6)
    pl.when(c == 1)(far_halves)
    came(gv.at[0], ag_r.at[6])
    terms((1, 3))
    pl.when(c == 0)(far_halves)
    to_z(0)
    came(gv.at[2, 1], ag_r.at[7])
    terms((2,))

    HB = 256

    def head_copy(n):
        rows = pl.ds(pl.multiple_of(n * HB, HB), HB)
        return pltpu.make_async_copy(head.at[rows], out_head.at[rows], head_sem)

    def head_part(low, high):
        @pl.loop(low, high)
        def _(n):
            rows = pl.ds(pl.multiple_of(n * HB, HB), HB)
            ga = gv[:, :, :, rows].reshape(8 * TOK, HB)
            hb = hv[...].reshape(8 * TOK, FEAT)
            head[rows, :] = mm(ga, hb, 0, 0).astype(BF16)
            head_copy(n).start()

    nh = VOCAB // HB
    head_part(0, 3)
    to_z(3)
    to_z(1)
    head_part(3, 5)
    to_z(2)
    head_part(5, nh)
    came(lossb.at[pl.ds(0, 7)], ls_r)
    loss = lossb[0]
    for k in range(1, 8):
        loss = loss + lossb[k]


    acc = zr[0].astype(F32)
    came(zr.at[pl.ds(1, NZ - 1)], z_r)
    for r in range(1, NZ):
        acc = acc + zr[r].astype(F32)
    out_small[0:24, :] = acc[0:24]
    out_small[24:32, :] = jnp.broadcast_to(loss * (1.0 / (8 * TOK)), (8, 128))

    gone(hv.at[0, 1], hs_sem.at[0])
    gone(hv.at[0], hs_sem.at[2])
    gone(hv.at[pl.ds(0, 2)], hs_sem.at[1])
    gone(psib, ss_sem)
    gone(enc_opp, rs_s.at[0])
    gone(enc_nb, rs_s.at[1])
    gone(psz.at[pl.ds(0, NZ * NX - 1)], pz_s)
    gone(lossb.at[pl.ds(0, 7)], ls_s)
    gone(gv.at[0, 0], ag_s.at[0])
    gone(gv.at[0, 0], ag_s.at[1])
    gone(gv.at[0, 0], ag_s.at[2])
    gone(gv.at[0, 0], ag_s.at[3])
    gone(gv.at[0], ag_s.at[4])
    gone(gv.at[0, 0], ag_s.at[5])
    gone(xr.at[pl.ds(1, 31)], x_s)
    gone(zr.at[pl.ds(1, NZ - 1)], z_s)
    pltpu.make_async_copy(head, out_head, head_sem).wait()


def per_device(hidden, head_weight, teacher_ids, teacher_logits):
    vm = pltpu.VMEM
    dma = pltpu.SemaphoreType.DMA
    scratch = [
        vm((TOK, K), jnp.int32),
        vm((TOK, K), F32),
        vm((VOCAB, FEAT), BF16),
        vm((NY, NC, TOK, FEAT), BF16),
        vm((NQ, NY, TOK, QC), F32),
        vm((NQ, NY, TOK, QC), F32),
        vm((NQ, NY, TOK, QC), F32),
        vm((NQ, TOK, QC), jnp.int16),
        vm((NQ, 2, TOK, QC), jnp.int16),
        vm((NQ, TOK, QC), jnp.int16),
        vm((NQ, 2, TOK, QC), jnp.int16),
        vm((TOK, K), F32),
        vm((TOK, NHI, 128), F32),
        vm((NHI, TOK, 128), F32),
        vm((NHI, TOK, 128), F32),
        vm((NZ * NX, 1, 128), F32),
        vm((8, 1, 128), F32),
        vm((NY, NC, TOK, VOCAB), BF16),
        vm((NY, NX, 2 * TOK, 128), BF16),
        vm((NY * NC * NX, TOK, 128), BF16),
        vm((NY, NC, 2, 32, 128), BF16),
        vm((NZ, 32, 128), BF16),
        vm((VOCAB, FEAT), BF16),
        dma((2,)), dma, dma, dma((3,)), dma((3,)), dma, dma((1 + 2 * NQ,)), dma((2,)), dma((NQ,)), dma((NQ,)),
        dma, dma, dma, dma, dma((6,)), dma((8,)), dma, dma((NY,)), dma, dma, dma,
        pltpu.SemaphoreType.REGULAR, pltpu.SemaphoreType.REGULAR, pltpu.SemaphoreType.REGULAR,
    ]
    hbm = pl.BlockSpec(memory_space=pltpu.HBM)
    anys = pl.BlockSpec(memory_space=pl.ANY)
    vmem = pl.BlockSpec(memory_space=pltpu.VMEM)
    small, head_grad = pl.pallas_call(
        kernel,
        out_shape=(
            pltpu.VMEM((32, 128), F32),
            pltpu.VMEM((VOCAB, FEAT), BF16),
        ),
        in_specs=[hbm, hbm, hbm, hbm],
        out_specs=(vmem, anys),
        scratch_shapes=scratch,
        compiler_params=pltpu.CompilerParams(
            collective_id=0, has_side_effects=True, vmem_limit_bytes=56 * 1024 * 1024
        ),
    )(hidden, head_weight, teacher_ids, teacher_logits)
    hidden_grad = jnp.concatenate([small[:24, :64], small[:24, 64:]], axis=0).astype(BF16)
    return hidden_grad, head_grad, small[24, 0]


def solution(mesh):
    in_specs = (P("dp", None), P("vocab", "dp"), P("dp", None), P("dp", None))
    out_specs = (P("dp", "vocab"), P("vocab", "dp"), P())
    return jax.shard_map(
        per_device, mesh=mesh, in_specs=in_specs, out_specs=out_specs, check_vma=False
    )
```

```python
import jax
import jax.numpy as jnp
from jax import lax
from jax.experimental import pallas as pl
from jax.experimental.pallas import tpu as pltpu
from jax.sharding import PartitionSpec as P

MESH = pl.DeviceIdType.MESH
F32 = jnp.float32
BF16 = jnp.bfloat16
soft_cap = 30.0

NY, NC, NX, NZ = 4, 2, 4, 16
TOK, D, K = 48, 4096, 256
FEAT = D // 8
VOCAB = 131072 // 64
NQ = 4
QC = VOCAB // NQ
NHI = VOCAB // 128
BEND = 48.0
LEVELS = 32767.0


def encode(x):
    return jnp.round(x * (LEVELS / (jnp.abs(x) + BEND))).astype(jnp.int32).astype(jnp.int16)


def decode(q):
    u = q.astype(jnp.int32).astype(F32)
    return u * (BEND / (LEVELS - jnp.abs(u)))


def mm(a, b, ca, cb):
    return lax.dot_general(a, b, (((ca,), (cb,)), ((), ())), preferred_element_type=F32)


def kernel(
    hidden, weight, ids_in, logits_in, out_small, out_head,
    ids, logits, wv, hv, psib, pown, srecv, enc_opp, enc_nb, in_opp, in_nb,
    prob, tgt, es, om, psz, lossb, gv, xs, xr, zs, zr, head,
    id_sem, w_sem, own_sem, hs_sem, hr_sem, ss_sem, sr_sem, rs_s, rs_opp, rs_nb,
    pz_s, pz_r, ls_s, ls_r, ag_s, ag_r, x_s, x_r, z_s, z_r, head_sem, near2, near4, near8,
):
    me = lax.axis_index("dp")
    vo = lax.axis_index("vocab")
    y, c = me // 2, me % 2
    z, x = vo // NX, vo % NX

    def dp_dev(o, cx):
        return {"dp": ((y + o) % NY) * 2 + (c + cx) % 2, "vocab": vo}

    def x_dev(r):
        return {"dp": me, "vocab": z * NX + (x + r) % NX}

    def z_dev(zz):
        return {"dp": me, "vocab": zz * NX + x}

    def rc(src, dst, ssem, rsem, dev):
        return pltpu.make_async_remote_copy(
            src_ref=src, dst_ref=dst, send_sem=ssem, recv_sem=rsem, device_id=dev, device_id_type=MESH
        )


    def came(ref, sem):
        rc(ref, ref, hs_sem.at[0], sem, dp_dev(0, 1)).wait_recv()

    def gone(ref, sem):
        rc(ref, ref, sem, hr_sem.at[0], dp_dev(0, 1)).wait_send()

    barrier = pltpu.get_barrier_semaphore()

    def greet(dev):
        pl.semaphore_signal(barrier, inc=1, device_id=dev, device_id_type=MESH)

    for o in range(NY):
        for cx in range(NC):
            if o or cx:
                greet(dp_dev(o, cx))
    for r in range(1, NX):
        greet(x_dev(r))
    for r in (1, 2, NZ - 2, NZ - 1):
        greet(z_dev((z + r) % NZ))

    w_copy = pltpu.make_async_copy(weight, wv, w_sem)
    own_h = pltpu.make_async_copy(hidden.at[:, pl.ds(pl.multiple_of(me * FEAT, FEAT), FEAT)], hv.at[0, 0], own_sem)
    own_h.start()
    id_copies = [
        pltpu.make_async_copy(ids_in, ids, id_sem.at[0]), pltpu.make_async_copy(logits_in, logits, id_sem.at[1])
    ]
    for w in id_copies:
        w.start()
    w_copy.start()

    pl.semaphore_wait(barrier, 7 + (NX - 1) + 4)

    def tell(sem, *steps):
        for step in steps:
            for r in (step, NZ - step):
                pl.semaphore_signal(sem, inc=1, device_id=z_dev((z + r) % NZ), device_id_type=MESH)


    def hidden_copy(o, cx):
        dev = dp_dev(o, cx)
        back = (-o) % NY
        cols = pl.ds(pl.multiple_of(dev["dp"] * FEAT, FEAT), FEAT)
        n = (0, 1, 2, 1)[o]
        return rc(hidden.at[:, cols], hv.at[back, cx], hs_sem.at[n], hr_sem.at[n], dev)

    for o, cx in ((2, 0), (2, 1), (0, 1)):
        hidden_copy(o, cx).start()
    tell(near2, 1, 2)
    for r in range(1, NX):
        pl.semaphore_signal(near2, inc=1, device_id=x_dev(r), device_id_type=MESH)

    for w in id_copies:
        w.wait()
    lg = logits[...]
    logp = lg - jnp.log(jnp.sum(jnp.exp(lg), axis=1, keepdims=True))
    pr = jnp.exp(logp)
    prob[...] = pr
    entropy = jnp.sum(pr * logp, axis=1, keepdims=True)

    first = vo * VOCAB
    rows16 = lax.broadcasted_iota(jnp.int32, (NHI, K), 0)
    rows128 = lax.broadcasted_iota(jnp.int32, (128, K), 0)

    def target_tokens(n):
        for k in range(4):
            t = n * 4 + k
            place = ids[pl.ds(t, 1), :] - first
            p = prob[pl.ds(t, 1), :]
            a = jnp.where((place >> 7) == rows16, p, 0.0)
            a1 = a.astype(BF16)
            rest = a - a1.astype(F32)
            a2 = rest.astype(BF16)
            a3 = (rest - a2.astype(F32)).astype(BF16)
            b = jnp.where((place & 127) == rows128, 1.0, 0.0).astype(BF16)
            both = mm(jnp.concatenate([a1, a2, a3], axis=0), b, 1, 1)
            tgt[t] = both[0:NHI] + both[NHI:2 * NHI] + both[2 * NHI:3 * NHI]

    pl.loop(0, 8)(target_tokens)
    for o, cx in ((1, 0), (3, 0), (1, 1), (3, 1)):
        hidden_copy(o, cx).start()

    place_of = (0, 2, 1, 3)

    def partial_logits(q, offsets):
        hb = jnp.concatenate([hv[o].reshape(NC * TOK, FEAT) for o in offsets], axis=0)
        part = mm(hb, wv[pl.ds(pl.multiple_of(q * QC, QC), QC), :], 1, 1)
        for n, o in enumerate(offsets):
            pown[q, place_of[o]] = part[2 * n * TOK:(2 * n + 1) * TOK]
            psib[q, place_of[o]] = part[(2 * n + 1) * TOK:(2 * n + 2) * TOK]

    def sib_copy(q, offsets):
        places = pl.ds(place_of[offsets[0]], len(offsets))
        n = 0 if offsets == (0,) else 1 + q + NQ * (len(offsets) - 1)
        return rc(psib.at[q, places], srecv.at[q, places], ss_sem, sr_sem.at[n], dp_dev(0, 1))

    def q_of(s):
        return (s % 2) * 2 + s // 2

    def way(q):
        return 1 + 2 * (q // 2)

    def opp_copy(q):
        return rc(enc_opp.at[q], in_opp.at[q], rs_s.at[0], rs_opp.at[q], dp_dev(way(q), 0))

    def nb_copy(q, o):
        slot, back = o // 2, 1 - o // 2
        return rc(enc_nb.at[q, slot], in_nb.at[q, back], rs_s.at[1], rs_nb.at[q], dp_dev(o, 0))

    w_copy.wait()
    own_h.wait()
    came(hv.at[0, 1], hr_sem.at[0])

    @pl.loop(0, NQ)
    def _(q):
        partial_logits(q, (0,))
        sib_copy(q, (0,)).start()

    pl.loop(8, TOK // 4)(target_tokens)
    pl.semaphore_wait(near2, 4 + NX - 1)
    tell(near4, 4)
    came(hv.at[2], hr_sem.at[2])

    @pl.loop(0, NQ)
    def _(s):
        q = q_of(s)
        partial_logits(q, (2,))
        sib_copy(q, (2,)).start()


    @pl.loop(0, NQ)
    def _(s):
        q = q_of(s)
        sib_copy(q, (2,)).wait_recv()
        enc_opp[q] = encode(pown[q, 1] + srecv[q, 1])
        opp_copy(q).start()

    came(hv.at[pl.ds(0, 2)], hr_sem.at[1])

    @pl.loop(0, NQ + 3)
    def _(s):
        @pl.when(s < NQ)
        def _():
            q = q_of(s)
            partial_logits(q, (1, 3))
            sib_copy(q, (1, 3)).start()

        @pl.when(jnp.logical_and(s > 1, s <= NQ + 1))
        def _():
            q = q_of(s - 2)
            sib_copy(q, (1, 3)).wait_recv()
            o = 4 - way(q)
            enc_nb[q, o // 2] = encode(pown[q, 2 + o // 2] + srecv[q, 2 + o // 2])
            nb_copy(q, o).start()

        @pl.when(s > 2)
        def _():
            q = q_of(s - 3)
            opp_copy(q).wait_recv()
            o = way(q)
            enc_nb[q, o // 2] = encode(pown[q, 2 + o // 2] + srecv[q, 2 + o // 2] + decode(in_opp[q]))
            nb_copy(q, o).start()

    pl.semaphore_wait(near4, 2)
    tell(near8, 4)
    tot = jnp.zeros((TOK, 128), F32)
    crs = jnp.zeros((TOK, 128), F32)
    came(srecv.at[:, 0], sr_sem.at[0])
    for s in range(NQ):
        q = q_of(s)
        came(in_nb.at[q], rs_nb.at[q])
        for k in range(QC // 128):
            cols = slice(k * 128, (k + 1) * 128)
            hi = q * (QC // 128) + k
            raw = (
                pown[q, 0, :, cols] + srecv[q, 0, :, cols]
                + decode(in_nb[q, 0, :, cols]) + decode(in_nb[q, 1, :, cols])
            )
            squash = jnp.tanh(raw * (1.0 / soft_cap))
            student = soft_cap * squash
            expo = jnp.exp(student)
            es[hi] = expo
            om[hi] = 1.0 - squash * squash
            tot = tot + expo
            crs = crs + tgt[:, hi, :] * student

    lane = lax.broadcasted_iota(jnp.int32, (TOK, 128), 1)
    row = lax.broadcasted_iota(jnp.int32, (TOK, 128), 0)
    mine = jnp.where(lane == row, jnp.sum(tot, axis=1, keepdims=True), 0.0) + jnp.where(
        lane == row + 64, jnp.sum(crs, axis=1, keepdims=True), 0.0
    )
    psz[vo] = jnp.sum(mine, axis=0, keepdims=True)
    pl.semaphore_wait(near8, 2)

    @pl.loop(0, NZ * NX - 1)
    def _(n):
        there = (vo + NZ * NX // 2 + (1 - 2 * (n % 2)) * ((n + 1) // 2)) % (NZ * NX)
        rc(psz.at[vo], psz.at[vo], pz_s, pz_r, {"dp": me, "vocab": there}).start()

    came(psz.at[pl.ds(0, NZ * NX - 1)], pz_r)
    sums = jnp.sum(psz[...], axis=0)
    sums = jnp.broadcast_to(sums, (TOK, 128))
    total = jnp.sum(jnp.where(lane == row, sums, 0.0), axis=1, keepdims=True)
    cross = jnp.sum(jnp.where(lane == row + 64, sums, 0.0), axis=1, keepdims=True)
    inv = 1.0 / total
    for hi in range(NHI):
        g = (es[hi] * inv - tgt[:, hi, :]) * om[hi]
        gv[0, 0, :, hi * 128:(hi + 1) * 128] = g.astype(BF16)

    half = [pl.ds(0, VOCAB // 2), pl.ds(VOCAB // 2, VOCAB // 2)]
    half += [pl.ds(n * (VOCAB // 4), VOCAB // 4) for n in range(4)]

    def pass_on(o, h, do, dcx, ssem, rsem):
        back = (o - do) % NY
        src = gv.at[o, 0] if h is None else gv.at[o, 0, :, half[h]]
        dst = gv.at[back, dcx] if h is None else gv.at[back, dcx, :, half[h]]
        rc(src, dst, ag_s.at[ssem], ag_r.at[rsem], dp_dev(do, dcx)).start()

    pass_on(0, 2, 1, 0, 0, 0)
    pass_on(0, 4, 3, 0, 0, 1)
    pass_on(0, 3, 1, 0, 0, 8)
    pass_on(0, 5, 3, 0, 0, 9)
    pass_on(0, None, 0, 1, 1, 2)

    token_loss = entropy - cross + jnp.log(total)
    lossb[me] = jnp.broadcast_to(jnp.sum(token_loss, axis=0, keepdims=True), (1, 128))
    for o in range(NY):
        for cx in range(NC):
            if o or cx:
                dev = dp_dev(o, cx)
                rc(lossb.at[me], lossb.at[me], ls_s, ls_r, dev).start()

    def send_terms(o):
        for cx in range(NC):
            for r in range(NX):
                there = (x + r) % NX
                src = xs.at[o, there, pl.ds(cx * TOK, TOK)]
                slot = ((-o) % NY * NC + cx) * NX + (-r) % NX
                if o or cx or r:
                    dev = {"dp": dp_dev(o, cx)["dp"], "vocab": z * NX + there}
                    rc(src, xr.at[slot], x_s, x_r.at[(-o) % NY], dev).start()
                else:
                    xr[0] = xs[0, x, 0:TOK]

    def terms(offsets):
        ga = jnp.concatenate([gv[o].reshape(NC * TOK, VOCAB) for o in offsets], axis=0)
        part = [mm(ga, wv[:, n * 256:(n + 1) * 256], 1, 0) for n in range(2)]
        for n, o in enumerate(offsets):
            rows = slice(n * NC * TOK, (n + 1) * NC * TOK)
            for m in range(NX):
                cols = slice(m * 64, (m + 1) * 64)
                piece = jnp.concatenate([part[0][rows, cols], part[1][rows, cols]], axis=1)
                xs[o, m] = piece.astype(BF16)
            send_terms(o)

    def to_z(o):
        low = o * NC * NX
        came(xr.at[pl.ds(low, 8)] if o else xr.at[pl.ds(1, 7)], x_r.at[o])
        for cx in range(NC):
            val = xr[low + cx * NX].astype(F32)
            for r in range(1, NX):
                val = val + xr[low + cx * NX + r].astype(F32)
            gap = jnp.zeros((8, 128), F32)
            for h in range(2):
                cols = slice(h * 64, (h + 1) * 64)
                part = jnp.concatenate([val[0:24, cols], val[24:48, cols]], axis=1)
                zs[o, cx, h] = jnp.concatenate([part, gap], axis=0).astype(BF16)
                zd = 2 * dp_dev(o, cx)["dp"] + h
                r = (z - zd + NZ) % NZ
                here = r == 0

                @pl.when(jnp.logical_not(here))
                def _():
                    rc(zs.at[o, cx, h], zr.at[r], z_s, z_r, z_dev(zd)).start()

                @pl.when(here)
                def _():
                    zr[0] = zs[o, cx, h]

    def second_halves():
        pass_on(0, 1, 1, 0, 2, 3)
        pass_on(0, 0, 3, 0, 2, 3)

    def far_halves():
        for h in range(2):
            came(gv.at[2, 0, :, half[h]], ag_r.at[4 + h])
            pass_on(2, h, 0, 1, 5, 7)


    def terms_own():
        came(gv.at[0, 1], ag_r.at[2])
        terms((0,))

    pl.when(c == 1)(second_halves)

    @pl.when(c == 0)
    def _():
        terms_own()
        second_halves()

    for n in range(2):
        came(gv.at[3, 0, :, half[2 + n]], ag_r.at[8 * n])
        pass_on(3, 2 + n, 1, 0, 3, 4)
        came(gv.at[1, 0, :, half[4 + n]], ag_r.at[1 + 8 * n])
        pass_on(1, 4 + n, 3, 0, 3, 5)
    pass_on(3, 0, 0, 1, 4, 6)
    pass_on(1, 1, 0, 1, 4, 6)
    pl.when(c == 1)(terms_own)
    came(gv.at[0, 0], ag_r.at[3])
    pass_on(3, 1, 0, 1, 4, 6)
    pass_on(1, 0, 0, 1, 4, 6)
    pl.when(c == 1)(far_halves)
    came(gv.at[0], ag_r.at[6])
    terms((1, 3))
    pl.when(c == 0)(far_halves)
    to_z(0)
    came(gv.at[2, 1], ag_r.at[7])
    terms((2,))

    HB = 256

    def head_copy(n):
        rows = pl.ds(pl.multiple_of(n * HB, HB), HB)
        return pltpu.make_async_copy(head.at[rows], out_head.at[rows], head_sem)

    def head_part(low, high):
        @pl.loop(low, high)
        def _(n):
            rows = pl.ds(pl.multiple_of(n * HB, HB), HB)
            ga = gv[:, :, :, rows].reshape(8 * TOK, HB)
            hb = hv[...].reshape(8 * TOK, FEAT)
            head[rows, :] = mm(ga, hb, 0, 0).astype(BF16)
            head_copy(n).start()

    nh = VOCAB // HB
    head_part(0, 3)
    to_z(3)
    to_z(1)
    head_part(3, 5)
    to_z(2)
    head_part(5, nh)
    came(lossb.at[pl.ds(0, 7)], ls_r)
    loss = lossb[0]
    for k in range(1, 8):
        loss = loss + lossb[k]


    acc = zr[0].astype(F32)
    came(zr.at[pl.ds(1, NZ - 1)], z_r)
    for r in range(1, NZ):
        acc = acc + zr[r].astype(F32)
    out_small[0:24, :] = acc[0:24]
    out_small[24:32, :] = jnp.broadcast_to(loss * (1.0 / (8 * TOK)), (8, 128))

    gone(hv.at[0, 1], hs_sem.at[0])
    gone(hv.at[0], hs_sem.at[2])
    gone(hv.at[pl.ds(0, 2)], hs_sem.at[1])
    gone(psib, ss_sem)
    gone(enc_opp, rs_s.at[0])
    gone(enc_nb, rs_s.at[1])
    gone(psz.at[pl.ds(0, NZ * NX - 1)], pz_s)
    gone(lossb.at[pl.ds(0, 7)], ls_s)
    gone(gv.at[0, 0], ag_s.at[0])
    gone(gv.at[0, 0], ag_s.at[1])
    gone(gv.at[0, 0], ag_s.at[2])
    gone(gv.at[0, 0], ag_s.at[3])
    gone(gv.at[0], ag_s.at[4])
    gone(gv.at[0, 0], ag_s.at[5])
    gone(xr.at[pl.ds(1, 31)], x_s)
    gone(zr.at[pl.ds(1, NZ - 1)], z_s)
    pltpu.make_async_copy(head, out_head, head_sem).wait()


def per_device(hidden, head_weight, teacher_ids, teacher_logits):
    vm = pltpu.VMEM
    dma = pltpu.SemaphoreType.DMA
    scratch = [
        vm((TOK, K), jnp.int32),
        vm((TOK, K), F32),
        vm((VOCAB, FEAT), BF16),
        vm((NY, NC, TOK, FEAT), BF16),
        vm((NQ, NY, TOK, QC), F32),
        vm((NQ, NY, TOK, QC), F32),
        vm((NQ, NY, TOK, QC), F32),
        vm((NQ, TOK, QC), jnp.int16),
        vm((NQ, 2, TOK, QC), jnp.int16),
        vm((NQ, TOK, QC), jnp.int16),
        vm((NQ, 2, TOK, QC), jnp.int16),
        vm((TOK, K), F32),
        vm((TOK, NHI, 128), F32),
        vm((NHI, TOK, 128), F32),
        vm((NHI, TOK, 128), F32),
        vm((NZ * NX, 1, 128), F32),
        vm((8, 1, 128), F32),
        vm((NY, NC, TOK, VOCAB), BF16),
        vm((NY, NX, 2 * TOK, 128), BF16),
        vm((NY * NC * NX, TOK, 128), BF16),
        vm((NY, NC, 2, 32, 128), BF16),
        vm((NZ, 32, 128), BF16),
        vm((VOCAB, FEAT), BF16),
        dma((2,)), dma, dma, dma((3,)), dma((3,)), dma, dma((1 + 2 * NQ,)), dma((2,)), dma((NQ,)), dma((NQ,)),
        dma, dma, dma, dma, dma((6,)), dma((10,)), dma, dma((NY,)), dma, dma, dma,
        pltpu.SemaphoreType.REGULAR, pltpu.SemaphoreType.REGULAR, pltpu.SemaphoreType.REGULAR,
    ]
    hbm = pl.BlockSpec(memory_space=pltpu.HBM)
    anys = pl.BlockSpec(memory_space=pl.ANY)
    vmem = pl.BlockSpec(memory_space=pltpu.VMEM)
    small, head_grad = pl.pallas_call(
        kernel,
        out_shape=(
            pltpu.VMEM((32, 128), F32),
            pltpu.VMEM((VOCAB, FEAT), BF16),
        ),
        in_specs=[hbm, hbm, hbm, hbm],
        out_specs=(vmem, anys),
        scratch_shapes=scratch,
        compiler_params=pltpu.CompilerParams(
            collective_id=0, has_side_effects=True, vmem_limit_bytes=56 * 1024 * 1024
        ),
    )(hidden, head_weight, teacher_ids, teacher_logits)
    hidden_grad = jnp.concatenate([small[:24, :64], small[:24, 64:]], axis=0).astype(BF16)
    return hidden_grad, head_grad, small[24, 0]


def solution(mesh):
    in_specs = (P("dp", None), P("vocab", "dp"), P("dp", None), P("dp", None))
    out_specs = (P("dp", "vocab"), P("vocab", "dp"), P())
    return jax.shard_map(
        per_device, mesh=mesh, in_specs=in_specs, out_specs=out_specs, check_vma=False
    )
```
